32 devices in a mesh: slab: 8 (over y, x, core), xy: 4 (over z).
Axes of the slice: x: 2, y: 2, z: 4, core: 2. Of those that a mesh axis runs over, the one named last changes fastest.
Arguments:
- volume: float32 [16, 32, 512], P('slab', 'xy'), may hold values from 0 to 1
- footprint: bfloat16 [16, 32, 4, 2, 128, 256], P('slab', 'xy'), may hold values from 0.049804688 to 1
- tile_block: int32 [16, 32, 4, 2], P('slab', 'xy'), may hold values from 0 to 511, as said below
- tile_cells: int32 [16, 32, 4, 2], P('slab', 'xy'), may hold values from 1 to 256, as said below
- measured: float32 [2, 131072], replicated, may hold values from 0 to 128
Outputs:
- updated: float32 [16, 32, 512], P('slab', 'xy')
- correction: float32 [2, 131072], P(None, ('slab', 'xy'))
The draws below stay inside these ranges and needn't reach their ends.
Inputs may be any that keep to these rules, and one draw needn't show every extreme that they name: `tile_cells`: at least one tile of some view has all 256 cells live. `tile_block`: A tile's block lies in detector row about plane * 4, off by at most one below and 4 above (within the detector); its column block follows the tile's place along the row for even views and the row's place in the plane for odd views, off by at most one.
All inputs are finite; a program needn't handle non-finite values.
Results may differ from the reference program's by a relative error of at most 0.0003.
Values may be sent and summed in bfloat16 or wider, within the bound.
No kernel may reach another device: no remote copies, remote signals or barrier semaphores. Data moves between devices by JAX's collectives and lax.ppermute only.
A program may use at most 64 MiB of HBM per device.

```python
import jax
import jax.numpy as jnp
from jax import lax

PLANES = 16
NX = 32
NY = 512
TV = 128
NYB = 4
VIEWS = 2
DROWS = 64
DCOLS = 2048
DET = 131072
TD = 256
NB = 512


def draw_tile_cells(key, part):
    shape = (PLANES, NX, NYB, VIEWS)
    first, second = jax.random.split(jax.random.fold_in(key, 11))
    cells = jax.random.randint(first, shape, 1, TD + 1).reshape(-1)
    spot = jax.random.randint(second, (), 0, cells.shape[0])
    cells = jnp.where(jnp.arange(cells.shape[0]) == spot, TD, cells)
    return cells.reshape(shape).astype(jnp.int32)


def draw_tile_block(key, part):
    shape = (PLANES, NX, NYB, VIEWS)
    key_row, key_col = jax.random.split(jax.random.fold_in(key, 23))
    per_row = DCOLS // TD
    lift = max(DROWS // PLANES, 1)
    plane = jnp.arange(PLANES, dtype=jnp.int32)[:, None, None, None]
    xrow = jnp.arange(NX, dtype=jnp.int32)[None, :, None, None]
    tile = jnp.arange(NYB, dtype=jnp.int32)[None, None, :, None]
    view = jnp.arange(VIEWS, dtype=jnp.int32)[None, None, None, :]
    det_row = plane * DROWS // PLANES + jax.random.randint(key_row, shape, -1, lift + 1)
    det_row = jnp.clip(det_row, 0, DROWS - 1)
    along = jnp.where(view % 2 == 0, tile * per_row // NYB, xrow * per_row // NX)
    det_col = jnp.clip(along + jax.random.randint(key_col, shape, -1, 2), 0, per_row - 1)
    return (det_row * per_row + det_col).astype(jnp.int32)


def levels(rng, dims, pieces, smallest, top_value):
    def one(position, blocks):
        steps = jax.random.uniform(jax.random.fold_in(jax.random.fold_in(rng, 6), position), (blocks,), jnp.float32, smallest / len(pieces), top_value / len(pieces))
        return jnp.repeat(jnp.exp(steps), dims[position] // blocks).reshape((-1,) + (1,) * (len(dims) - position - 1))

    gain = one(*pieces[0])
    for cut in pieces[1:]:
        gain = gain * one(*cut)
    return gain


def setup_inputs(seed: int = 0) -> dict:
    key_list = jax.random.split(jax.random.key(seed), 6)
    volume = jnp.clip(1.0 * jax.random.uniform(key_list[0], (PLANES, NX, NY), jnp.float32) ** levels(key_list[0], (PLANES, NX, NY), ((0, 8), (1, 4)), -0.2, 0.2), 0.0, 1.0)
    footprint = jnp.clip(0.049804688 + 0.9501953 * jax.random.uniform(key_list[1], (PLANES, NX, NYB, VIEWS, TV, TD), jnp.float32) ** levels(key_list[1], (PLANES, NX, NYB, VIEWS, TV, TD), ((0, 8), (1, 4)), -0.2, 0.2), 0.049804688, 1.0).astype(jnp.bfloat16)
    tile_block = draw_tile_block(jax.random.fold_in(key_list[5], 71), 0)
    tile_cells = draw_tile_cells(jax.random.fold_in(key_list[5], 71), 0)
    measured = jnp.clip(jax.random.uniform(key_list[4], (VIEWS, DET), jnp.float32, 0.0, 128.0), 0.0, 128.0)
    return dict(volume=volume, footprint=footprint, tile_block=tile_block, tile_cells=tile_cells, measured=measured)


RELAX = 1.0
TV_RATE = 0.8
SMOOTHING = 0.01

def masked_plane(foot_plane, cells_plane):
    lane = jnp.arange(TD, dtype=jnp.int32)
    live = lane[None, None, None, :] < cells_plane[:, :, :, None]
    return jnp.where(live[:, :, :, None, :], foot_plane, jnp.zeros((), jnp.bfloat16))

def tv_slope(padded):
    base = padded[:-1, :-1, :-1]
    diff_a = padded[1:, :-1, :-1] - base
    diff_b = padded[:-1, 1:, :-1] - base
    diff_e = padded[:-1, :-1, 1:] - base
    size = jnp.sqrt(diff_a * diff_a + diff_b * diff_b + diff_e * diff_e + SMOOTHING)
    unit_a = diff_a / size
    unit_b = diff_b / size
    unit_e = diff_e / size
    total = unit_a + unit_b + unit_e
    return -total[1:, 1:, 1:] + unit_a[:-1, 1:, 1:] + unit_b[1:, :-1, 1:] + unit_e[1:, 1:, :-1]

def reference(volume, footprint, tile_block, tile_cells, measured):
    blocks = jnp.arange(NB, dtype=jnp.int32)

    def forward(carry, inputs):
        vol_plane, foot_plane, block_plane, cells_plane = inputs
        weights = masked_plane(foot_plane, cells_plane).astype(jnp.float32)
        voxels = vol_plane.astype(jnp.bfloat16).astype(jnp.float32).reshape(NX, NYB, TV)
        contrib = jnp.einsum('abj,abvjc->abvc', voxels, weights)
        rays = lax.optimization_barrier(jnp.sum(weights, axis=3))
        onehot = (block_plane[:, :, :, None] == blocks).astype(jnp.float32)
        proj = jnp.einsum('abvn,abvc->vnc', onehot, contrib, precision=lax.Precision.HIGHEST)
        ray = jnp.einsum('abvn,abvc->vnc', onehot, rays, precision=lax.Precision.HIGHEST)
        return ((carry[0] + proj, carry[1] + ray), None)
    start = jnp.zeros((VIEWS, NB, TD), jnp.float32)
    (projected, ray_weight), _ = lax.scan(forward, (start, start), (volume, footprint, tile_block, tile_cells))
    projected = projected.reshape(VIEWS, DET)
    ray_weight = ray_weight.reshape(VIEWS, DET)
    correction = (measured - projected) / jnp.maximum(ray_weight, 1.0)
    correction_b = correction.astype(jnp.bfloat16).reshape(VIEWS, NB, TD)
    view_ids = jnp.arange(VIEWS, dtype=jnp.int32)

    def backward(inputs):
        foot_plane, block_plane, cells_plane = inputs
        weights = masked_plane(foot_plane, cells_plane).astype(jnp.float32)
        picked = correction_b[view_ids[None, None, :], block_plane].astype(jnp.float32)
        back = jnp.einsum('abvjc,abvc->abj', weights, picked)
        column = lax.optimization_barrier(jnp.sum(weights, axis=(2, 4)))
        return (back / column).reshape(NX, NY)
    shift = lax.map(backward, (footprint, tile_block, tile_cells))
    sart = jnp.maximum(volume + RELAX * shift, 0.0)
    step_gap = sart - volume
    update_norm = jnp.sqrt(jnp.sum(step_gap * step_gap))
    current = sart
    for turn in range(2):
        slope = tv_slope(jnp.pad(current, 1))
        scale = jnp.sqrt(jnp.sum(slope * slope) + 1e-06)
        current = current - TV_RATE * update_norm / scale * slope
    return (current, correction)
```

```python
import functools

import jax
import jax.numpy as jnp
from jax import lax
from jax.experimental import pallas as pl
from jax.experimental.pallas import tpu as pltpu
from jax.sharding import PartitionSpec as P

RELAX = 1.0
TV_RATE = 0.8
SMOOTHING = 0.01
DCOLS = 2048
VMEM_BYTES = 32 * 1024 * 1024


class Plan:
    def __init__(self, slabs, bands, views, nblocks, tdet):
        self.slabs, self.bands, self.views = slabs, bands, views
        self.per_row = DCOLS // tdet
        self.own = nblocks // (slabs * bands)
        self.slab_own = nblocks // slabs
        self.halo = self.per_row
        self.local = self.slab_own + 2 * self.halo
        self.drows = self.local // self.per_row
        narrow = self.per_row // bands
        own_rows = self.own % self.per_row == 0
        self.narrow = narrow if narrow >= 1 and narrow * bands == self.per_row and own_rows else 0
        self.width = [
            self.narrow + 2 if v % 2 and self.narrow else self.per_row for v in range(views)
        ]
        self.base = [sum(self.width[:v]) * self.drows for v in range(views)]
        self.total = sum(self.width) * self.drows

    def first_column(self, v, band):
        return band * self.narrow - 1 if v % 2 and self.narrow else 0


def shift_all(cells, axis, step):
    count = lax.axis_size(axis)
    return lax.ppermute(cells, axis, [(i, (i + step) % count) for i in range(count)])


def swap_all(cells, axis, flip):
    count = lax.axis_size(axis)
    return lax.ppermute(cells, axis, [(i, i ^ flip) for i in range(count)])


def block_index(plan, v, block, slab, band):
    local = block - slab * plan.slab_own + plan.halo
    row = lax.div(local, plan.per_row)
    column = lax.rem(local, plan.per_row) - plan.first_column(v, band)
    index = row * plan.width[v] + column
    return jnp.clip(index, 0, plan.width[v] * plan.drows - 1)


def project_kernel(plan, shape, vol_ref, foot_ref, block_ref, cells_ref, out_ref, acc, foot, sems):
    planes, rows, tiles, views, tvox, tdet = shape
    slab, band = lax.axis_index("slab"), lax.axis_index("xy")
    parts = sems.shape[0]
    step = rows * planes // parts

    def copy(n):
        p, r = n * step // rows, n * step % rows
        return pltpu.make_async_copy(
            foot_ref.at[p, pl.ds(r, step)], foot.at[p, pl.ds(r, step)], sems.at[n]
        )

    for n in range(parts):
        copy(n).start()
    acc[...] = jnp.zeros_like(acc)
    top = lax.broadcasted_iota(jnp.int32, (8, tvox), 0) == 0
    lane = lax.broadcasted_iota(jnp.int32, (8, tdet), 1)
    for n in range(parts):
        copy(n).wait()
        for p, r in [divmod(n * step + k, rows) for k in range(step)]:
            for t in range(tiles):
                voxels = vol_ref[p, r : r + 1, t * tvox : (t + 1) * tvox]
                left = jnp.where(top, jnp.broadcast_to(voxels, (8, tvox)), 1.0)
                left = left.astype(jnp.bfloat16)
                for v in range(views):
                    sums = jnp.dot(left, foot[p, r, t, v], preferred_element_type=jnp.float32)
                    sums = jnp.where(lane < cells_ref[p, r, t, v], sums, 0.0)
                    at = plan.base[v] + block_index(plan, v, block_ref[p, r, t, v], slab, band)
                    acc[at] += sums
    out_ref[0] = acc[:, 0, :]
    out_ref[1] = acc[:, 1, :]


def project(plan, volume, footprint, tile_block, tile_cells):
    shape = footprint.shape
    parts = shape[0] * shape[1]
    tdet = shape[-1]
    return pl.pallas_call(
        functools.partial(project_kernel, plan, shape),
        out_shape=jax.ShapeDtypeStruct((2, plan.total, tdet), jnp.float32),
        in_specs=[
            pl.BlockSpec(memory_space=pltpu.VMEM),
            pl.BlockSpec(memory_space=pl.ANY),
            pl.BlockSpec(memory_space=pltpu.SMEM),
            pl.BlockSpec(memory_space=pltpu.SMEM),
        ],
        out_specs=pl.BlockSpec(memory_space=pltpu.VMEM),
        scratch_shapes=[
            pltpu.VMEM((plan.total, 8, tdet), jnp.float32),
            pltpu.VMEM(shape, jnp.bfloat16),
            pltpu.SemaphoreType.DMA((parts,)),
        ],
        compiler_params=pltpu.CompilerParams(vmem_limit_bytes=VMEM_BYTES),
        name="project",
    )(volume, footprint, tile_block, tile_cells)


def back_kernel(
    plan, shape, vol_ref, foot_ref, block_ref, cells_ref, corr_ref, sart_ref, gap_ref, sums, foot, sems
):
    planes, rows, tiles, views, tvox, tdet = shape
    slab = lax.axis_index("slab")
    parts = sems.shape[0]
    step = rows * planes // parts

    def copy(n):
        p, r = n * step // rows, n * step % rows
        return pltpu.make_async_copy(
            foot_ref.at[p, pl.ds(r, step)], foot.at[p, pl.ds(r, step)], sems.at[n]
        )

    for n in range(parts):
        copy(n).start()
    top = lax.broadcasted_iota(jnp.int32, (8, tdet), 0) == 0
    lane = lax.broadcasted_iota(jnp.int32, (8, tdet), 1)
    for n in range(parts):
        copy(n).wait()
        for p, r in [divmod(n * step + k, rows) for k in range(step)]:
            for t in range(tiles):
                both = 0.0
                for v in range(views):
                    local = block_ref[p, r, t, v] - slab * plan.slab_own + plan.halo
                    local = jnp.clip(local, 0, plan.local - 1)
                    picked = jnp.broadcast_to(corr_ref[v, pl.ds(local, 1), :], (8, tdet))
                    left = jnp.where(top, picked, 1.0)
                    left = jnp.where(lane < cells_ref[p, r, t, v], left, 0.0).astype(jnp.bfloat16)
                    both += lax.dot_general(
                        left,
                        foot[p, r, t, v],
                        (((1,), (1,)), ((), ())),
                        preferred_element_type=jnp.float32,
                    )
                at = slice(t * tvox, (t + 1) * tvox)
                sums[0, p, r : r + 1, at] = both[0:1]
                sums[1, p, r : r + 1, at] = both[1:2]
    volume = vol_ref[...]
    sart = jnp.maximum(volume + RELAX * (sums[0] / sums[1]), 0.0)
    sart_ref[...] = sart
    gap = sart - volume
    gap_ref[...] = jnp.sum(gap * gap, axis=0)


def back_project(plan, volume, footprint, tile_block, tile_cells, corr):
    shape = footprint.shape
    parts = shape[0] * shape[1]
    return pl.pallas_call(
        functools.partial(back_kernel, plan, shape),
        out_shape=(
            jax.ShapeDtypeStruct(volume.shape, jnp.float32),
            jax.ShapeDtypeStruct(volume.shape[1:], jnp.float32),
        ),
        in_specs=[
            pl.BlockSpec(memory_space=pltpu.VMEM),
            pl.BlockSpec(memory_space=pl.ANY),
            pl.BlockSpec(memory_space=pltpu.SMEM),
            pl.BlockSpec(memory_space=pltpu.SMEM),
            pl.BlockSpec(memory_space=pltpu.VMEM),
        ],
        out_specs=(
            pl.BlockSpec(memory_space=pltpu.VMEM),
            pl.BlockSpec(memory_space=pltpu.VMEM),
        ),
        scratch_shapes=[
            pltpu.VMEM((2,) + volume.shape, jnp.float32),
            pltpu.VMEM(shape, jnp.bfloat16),
            pltpu.SemaphoreType.DMA((parts,)),
        ],
        compiler_params=pltpu.CompilerParams(vmem_limit_bytes=VMEM_BYTES),
        name="back_project",
    )(volume, footprint, tile_block, tile_cells, corr)


def part_of(plan, sums, v):
    size = plan.width[v] * plan.drows
    view = lax.slice_in_dim(sums, plan.base[v], plan.base[v] + size, axis=1)
    return view.reshape(2, plan.drows, plan.width[v], sums.shape[2])


def for_owner(plan, views, owner):
    pieces = []
    for view in views:
        width = view.shape[2]
        flat = view.reshape(2, -1, view.shape[3])
        own = plan.own * width // plan.per_row
        mine = lax.dynamic_slice_in_dim(flat, width + owner * own, own, 1)
        halo = lax.dynamic_slice_in_dim(
            flat, jnp.where(owner == 0, 0, flat.shape[1] - width), width, 1
        )
        pieces += [mine, halo]
    return jnp.concatenate(pieces, axis=1)


def place(plan, chunk, source):
    out, at = [], 0
    for v, width in enumerate(plan.width):
        size = plan.own * width // plan.per_row + width
        piece = lax.slice_in_dim(chunk, at, at + size, axis=1)
        at += size
        if width != plan.per_row:
            piece = piece.reshape(2, -1, width, chunk.shape[2])
            room = jnp.zeros((2, piece.shape[1], plan.per_row + 2, chunk.shape[2]), piece.dtype)
            room = lax.dynamic_update_slice_in_dim(room, piece, plan.narrow * source, 2)
            piece = room[:, :, 1:-1].reshape(2, -1, chunk.shape[2])
        out.append(piece)
    return jnp.stack(out, axis=1)


def total_of(parts):
    axes = ("slab", "xy")
    count = lax.axis_size(axes)
    row = jnp.concatenate(parts, axis=0)
    everyone = lax.all_to_all(jnp.broadcast_to(row[None], (count,) + row.shape), axes, 0, 0)
    return jnp.sum(everyone, axis=(0, 2))


def extended(cells, sides, width):
    for axis, dim in sides:
        head = lax.slice_in_dim(cells, 0, width, axis=dim)
        tail = lax.slice_in_dim(cells, cells.shape[dim] - width, cells.shape[dim], axis=dim)
        place_in = lax.axis_index(axis)
        before = jnp.where(place_in == 0, 0.0, shift_all(tail, axis, 1))
        after = jnp.where(place_in == lax.axis_size(axis) - 1, 0.0, shift_all(head, axis, -1))
        cells = jnp.concatenate([before, cells, after], axis=dim)
    return cells


def tv_slope(padded):
    base = padded[:-1, :-1, :-1]
    diff_a = padded[1:, :-1, :-1] - base
    diff_b = padded[:-1, 1:, :-1] - base
    diff_e = padded[:-1, :-1, 1:] - base
    size = jnp.sqrt(diff_a * diff_a + diff_b * diff_b + diff_e * diff_e + SMOOTHING)
    unit_a = diff_a / size
    unit_b = diff_b / size
    unit_e = diff_e / size
    total = unit_a + unit_b + unit_e
    return -total[1:, 1:, 1:] + unit_a[:-1, 1:, 1:] + unit_b[1:, :-1, 1:] + unit_e[1:, 1:, :-1]


def lanes_of(square):
    return jnp.sum(square.reshape(-1, 128), axis=0, keepdims=True)


def body(volume, footprint, tile_block, tile_cells, measured):
    planes, rows, ycells = volume.shape
    views, tdet = footprint.shape[3], footprint.shape[5]
    slabs, bands = lax.axis_size("slab"), lax.axis_size("xy")
    slab, band = lax.axis_index("slab"), lax.axis_index("xy")
    nblocks = measured.shape[1] // tdet
    plan = Plan(slabs, bands, views, nblocks, tdet)

    packed = project(plan, volume, footprint, tile_block, tile_cells)

    sums = [part_of(plan, packed, v) for v in range(views)]
    edge = 2
    low = jnp.concatenate([view[:, :edge] for view in sums], axis=2)
    high = jnp.concatenate([view[:, -edge:] for view in sums], axis=2)
    from_below = jnp.where(slab == 0, 0.0, shift_all(high, "slab", 1))
    from_above = jnp.where(slab == slabs - 1, 0.0, shift_all(low, "slab", -1))
    at = 0
    for v, width in enumerate(plan.width):
        view = sums[v]
        sums[v] = jnp.concatenate(
            [
                view[:, :edge] + from_below[:, :, at : at + width],
                view[:, edge:-edge],
                view[:, -edge:] + from_above[:, :, at : at + width],
            ],
            axis=1,
        )
        at += width

    total = place(plan, for_owner(plan, sums, band), band)
    for flip in range(1, bands):
        total = total + place(
            plan, swap_all(for_owner(plan, sums, band ^ flip), "xy", flip), band ^ flip
        )
    blocked = measured.reshape(views, nblocks, tdet)
    first = (slab * bands + band) * plan.own
    halo_at = jnp.where(
        band == 0, slab * plan.slab_own - plan.halo, (slab + 1) * plan.slab_own
    )
    seen = jnp.concatenate(
        [
            lax.dynamic_slice_in_dim(blocked, first, plan.own, 1),
            lax.dynamic_slice_in_dim(
                blocked, jnp.clip(halo_at, 0, nblocks - plan.halo), plan.halo, 1
            ),
        ],
        axis=1,
    )
    corrected = (seen - total[0]) / jnp.maximum(total[1], 1.0)
    correction = corrected[:, : plan.own].reshape(views, plan.own * tdet)

    rounded = corrected.astype(jnp.bfloat16)
    wide = jnp.zeros((views, plan.local, tdet), jnp.bfloat16)
    for flip in range(bands):
        piece = rounded if flip == 0 else swap_all(rounded, "xy", flip)
        source = band ^ flip
        wide = lax.dynamic_update_slice_in_dim(
            wide, piece[:, : plan.own], plan.halo + source * plan.own, 1
        )
        end = piece[:, plan.own :]
        wide = wide.at[:, : plan.halo].set(
            jnp.where(source == 0, end, wide[:, : plan.halo])
        )
        wide = wide.at[:, -plan.halo :].set(
            jnp.where(source == bands - 1, end, wide[:, -plan.halo :])
        )

    sart, gap = back_project(
        plan, volume, footprint, tile_block, tile_cells, wide.astype(jnp.float32)
    )

    rimmed = extended(sart, (("slab", 0), ("xy", 1)), 2)
    padded = jnp.pad(rimmed, ((0, 0), (0, 0), (2, 2)))
    slope_wide = tv_slope(padded)
    first_slope = slope_wide[1:-1, 1:-1, 1:-1]
    gap_square, first_square = total_of([lanes_of(gap), lanes_of(first_slope * first_slope)])
    update_norm = jnp.sqrt(gap_square)
    first_step = TV_RATE * update_norm / jnp.sqrt(first_square + 1e-06)
    wide = padded[1:-1, 1:-1, 1:-1] - first_step * slope_wide
    plane_ids = slab * planes + jnp.arange(planes + 2, dtype=jnp.int32) - 1
    row_ids = band * rows + jnp.arange(rows + 2, dtype=jnp.int32) - 1
    cell_ids = jnp.arange(ycells + 2, dtype=jnp.int32) - 1
    inside_plane = (plane_ids >= 0) & (plane_ids < slabs * planes)
    inside_row = (row_ids >= 0) & (row_ids < bands * rows)
    inside_cell = (cell_ids >= 0) & (cell_ids < ycells)
    inside = inside_plane[:, None, None] & inside_row[None, :, None] & inside_cell[None, None, :]
    wide = jnp.where(inside, wide, 0.0)
    second_slope = tv_slope(wide)
    (second_square,) = total_of([lanes_of(second_slope * second_slope)])
    second_step = TV_RATE * update_norm / jnp.sqrt(second_square + 1e-06)
    updated = wide[1:-1, 1:-1, 1:-1] - second_step * second_slope
    return (updated, correction)


def solution(mesh):
    placed = (
        P("slab", "xy", None),
        P("slab", "xy", None, None, None, None),
        P("slab", "xy", None, None),
        P("slab", "xy", None, None),
        P(),
    )
    return jax.shard_map(
        body,
        mesh=mesh,
        in_specs=placed,
        out_specs=(P("slab", "xy", None), P(None, ("slab", "xy"))),
        check_vma=False,
    )
```

```python
import functools

import jax
import jax.numpy as jnp
from jax import lax
from jax.experimental import pallas as pl
from jax.experimental.pallas import tpu as pltpu
from jax.sharding import PartitionSpec as P

RELAX = 1.0
TV_RATE = 0.8
SMOOTHING = 0.01
DCOLS = 2048
VMEM_BYTES = 32 * 1024 * 1024


class Plan:
    def __init__(self, slabs, bands, views, nblocks, tdet):
        self.slabs, self.bands, self.views, self.tdet = slabs, bands, views, tdet
        per_row = DCOLS // tdet
        own = nblocks // (slabs * bands)
        self.slab_own = nblocks // slabs
        self.halo = per_row
        self.unit = min(per_row, own)
        self.own_units = own // self.unit
        self.halo_units = per_row // self.unit
        self.units = self.slab_own // self.unit + 2 * self.halo_units
        self.chunk = self.own_units + self.halo_units
        narrow = per_row // bands
        fits = self.unit == per_row and narrow * bands == per_row and narrow + 2 < per_row
        self.narrow = narrow if fits else 0
        self.width = [
            self.narrow + 2 if v % 2 and self.narrow else self.unit for v in range(views)
        ]
        self.base = [2 * sum(self.width[:v]) for v in range(views)]
        self.lines = 2 * sum(self.width)

    def is_narrow(self, v):
        return self.width[v] != self.unit


def shift_all(cells, axis, step):
    count = lax.axis_size(axis)
    return lax.ppermute(cells, axis, [(i, (i + step) % count) for i in range(count)])


def swap_all(cells, axis, flip):
    count = lax.axis_size(axis)
    return lax.ppermute(cells, axis, [(i, i ^ flip) for i in range(count)])


def unit_of(plan, block, slab):
    local = jnp.clip(
        block - slab * plan.slab_own + plan.halo, 0, plan.units * plan.unit - 1
    )
    return lax.div(local, plan.unit), lax.rem(local, plan.unit)


def copy_all(pairs, sems):
    return [pltpu.make_async_copy(src, dst, sems.at[n]) for n, (src, dst) in enumerate(pairs)]


def project_kernel(
    plan, shape, vol_hbm, foot_hbm, block_hbm, cells_hbm, seen_hbm,
    out_ref, low_ref, high_ref, seen_ref, foot, acc, vol_ref, block_ref, cells_ref, seen, sems, small,
):
    planes, rows, tiles, views, tvox, tdet = shape
    slab, band = lax.axis_index("slab"), lax.axis_index("xy")
    parts = sems.shape[0]
    step = planes * rows // parts
    spans = [(n * step // rows, pl.ds(n * step % rows, step)) for n in range(parts)]
    span = plan.unit * tdet
    own_at = (slab * plan.bands + band) * plan.own_units
    halo_at = jnp.where(
        band == 0,
        slab * (plan.slab_own // plan.unit) - plan.halo_units,
        (slab + 1) * (plan.slab_own // plan.unit),
    )
    halo_at = jnp.clip(halo_at, 0, seen_hbm.shape[1] // span - plan.halo_units)
    own_at, halo_at = (pl.multiple_of(at * span, span) for at in (own_at, halo_at))
    own_size, halo_size = plan.own_units * span, plan.halo_units * span
    first = copy_all(
        [
            (block_hbm, block_ref),
            (cells_hbm, cells_ref),
            (vol_hbm, vol_ref),
            (seen_hbm.at[:, pl.ds(own_at, own_size)], seen.at[:, pl.ds(0, own_size)]),
            (seen_hbm.at[:, pl.ds(halo_at, halo_size)], seen.at[:, pl.ds(own_size, halo_size)]),
        ],
        small,
    )
    stream = copy_all([(foot_hbm.at[p, at], foot.at[p, at]) for p, at in spans], sems)
    for copy in first + stream:
        copy.start()
    acc[...] = jnp.zeros_like(acc)
    top = lax.broadcasted_iota(jnp.int32, (8, tvox), 0) == 0
    lane = lax.broadcasted_iota(jnp.int32, (8, tdet), 1)
    for copy in first:
        copy.wait()
    for v in range(views):
        for i in range(plan.chunk):
            for c in range(plan.unit):
                at = (i * plan.unit + c) * tdet
                seen_ref[v, i, c : c + 1, :] = seen[v : v + 1, at : at + tdet]
    starts = [plan.units * sum(plan.width[:v]) for v in range(views)]
    for n in range(parts):
        stream[n].wait()
        for p, r in [divmod(n * step + k, rows) for k in range(step)]:
            for t in range(tiles):
                voxels = vol_ref[p, r : r + 1, t * tvox : (t + 1) * tvox]
                left = jnp.where(top, jnp.broadcast_to(voxels, (8, tvox)), 1.0)
                left = left.astype(jnp.bfloat16)
                for v in range(views):
                    sums = jnp.dot(left, foot[p, r, t, v], preferred_element_type=jnp.float32)
                    sums = jnp.where(lane < cells_ref[p, t, v, r], sums, 0.0)
                    unit, column = unit_of(plan, block_ref[p, t, v, r], slab)
                    if plan.is_narrow(v):
                        column = column - (band * plan.narrow - 1)
                        column = jnp.clip(column, 0, plan.width[v] - 1)
                    acc[starts[v] + unit * plan.width[v] + column] += sums
    for unit in range(plan.units):
        for v in range(views):
            width = plan.width[v]
            at = starts[v] + unit * width
            for q in range(2):
                line = plan.base[v] + q * width
                out_ref[unit, line : line + width, :] = acc[at : at + width, q, :]
    edge = 2 * plan.halo_units
    low_ref[...] = out_ref[:edge]
    high_ref[...] = out_ref[plan.units - edge :]


def in_vmem(count):
    return [pl.BlockSpec(memory_space=pltpu.VMEM)] * count


def project(plan, volume, footprint, tile_block, tile_cells, measured):
    shape = footprint.shape
    planes, rows = shape[:2]
    views, tdet = plan.views, plan.tdet
    parts = 2 * planes if rows % 2 == 0 else planes
    operands = [
        pltpu.with_memory_space_constraint(operand, pltpu.HBM)
        for operand in (volume, footprint, tile_block, tile_cells, measured)
    ]
    border = (2 * plan.halo_units, plan.lines, tdet)
    return pl.pallas_call(
        functools.partial(project_kernel, plan, shape),
        out_shape=(
            jax.ShapeDtypeStruct((plan.units, plan.lines, tdet), jnp.float32),
            jax.ShapeDtypeStruct(border, jnp.float32),
            jax.ShapeDtypeStruct(border, jnp.float32),
            jax.ShapeDtypeStruct((views, plan.chunk, plan.unit, tdet), jnp.float32),
            pltpu.VMEM(shape, jnp.bfloat16),
        ),
        in_specs=[pl.BlockSpec(memory_space=pltpu.HBM)] * 5,
        out_specs=tuple(in_vmem(5)),
        scratch_shapes=[
            pltpu.VMEM((plan.units * sum(plan.width), 8, tdet), jnp.float32),
            pltpu.VMEM(volume.shape, jnp.float32),
            pltpu.SMEM(tile_block.shape, jnp.int32),
            pltpu.SMEM(tile_cells.shape, jnp.int32),
            pltpu.VMEM((views, plan.chunk * plan.unit * tdet), jnp.float32),
            pltpu.SemaphoreType.DMA((parts,)),
            pltpu.SemaphoreType.DMA((5,)),
        ],
        compiler_params=pltpu.CompilerParams(vmem_limit_bytes=VMEM_BYTES),
        name="project",
    )(*operands)


def share_kernel(plan, packed_ref, below_ref, above_ref, *rest):
    out_refs, total = rest[:-1], rest[-1]
    slab, band = lax.axis_index("slab"), lax.axis_index("xy")
    edge = 2 * plan.halo_units
    total[...] = packed_ref[...]
    total[:edge] += jnp.where(slab == 0, 0.0, below_ref[...])
    total[plan.units - edge :] += jnp.where(slab == plan.slabs - 1, 0.0, above_ref[...])
    for flip, out_ref in enumerate(out_refs):
        owner = band ^ flip
        for i in range(plan.own_units):
            out_ref[i] = total[plan.halo_units + owner * plan.own_units + i]
        halo = jnp.where(owner == 0, 0, plan.units - plan.halo_units)
        for i in range(plan.halo_units):
            out_ref[plan.own_units + i] = total[halo + i]


def shares(plan, packed, below, above):
    chunk = jax.ShapeDtypeStruct((plan.chunk,) + packed.shape[1:], jnp.float32)
    return pl.pallas_call(
        functools.partial(share_kernel, plan),
        out_shape=(chunk,) * plan.bands,
        in_specs=in_vmem(3),
        out_specs=tuple(in_vmem(plan.bands)),
        scratch_shapes=[pltpu.VMEM(packed.shape, jnp.float32)],
        compiler_params=pltpu.CompilerParams(vmem_limit_bytes=VMEM_BYTES // 4),
        name="shares",
    )(packed, below, above)


def correct_kernel(plan, seen_ref, *rest):
    parts, (exact_ref, rounded_ref) = rest[:-2], rest[-2:]
    band = lax.axis_index("xy")
    tdet, unit = plan.tdet, plan.unit
    rounded = []
    for v in range(plan.views):
        width = plan.width[v]
        for i in range(plan.chunk):
            sums = []
            for q in range(2):
                line = plan.base[v] + q * width
                total = 0.0
                for flip, part in enumerate(parts):
                    piece = part[i, line : line + width, :]
                    if plan.is_narrow(v):
                        room = jnp.zeros((unit - width, tdet), jnp.float32)
                        piece = jnp.concatenate([piece, room], axis=0)
                        first = (band ^ flip) * plan.narrow - 1
                        piece = pltpu.roll(piece, lax.rem(first + unit, unit), 0)
                    total = total + piece
                sums.append(total)
            corrected = (seen_ref[v, i] - sums[0]) / jnp.maximum(sums[1], 1.0)
            rounded.append(corrected)
            if i < plan.own_units:
                for c in range(unit):
                    at = (i * unit + c) * tdet
                    exact_ref[v : v + 1, at : at + tdet] = corrected[c : c + 1]
    rounded_ref[...] = jnp.concatenate(rounded, axis=0).astype(jnp.bfloat16)


def correct(plan, seen, parts):
    views, chunk, unit, tdet = seen.shape
    return pl.pallas_call(
        functools.partial(correct_kernel, plan),
        out_shape=(
            jax.ShapeDtypeStruct((views, plan.own_units * unit * tdet), jnp.float32),
            jax.ShapeDtypeStruct((views * chunk * unit, tdet), jnp.bfloat16),
        ),
        in_specs=in_vmem(1 + len(parts)),
        out_specs=tuple(in_vmem(2)),
        compiler_params=pltpu.CompilerParams(vmem_limit_bytes=VMEM_BYTES // 4),
        name="correct",
    )(seen, *parts)


def back_kernel(plan, shape, vol_any, foot, block_any, cells_any, *rest):
    parts, (out_ref, sums, corr, vol_ref, block_ref, cells_ref, small) = rest[:-7], rest[-7:]
    planes, rows, tiles, views, tvox, tdet = shape
    slab, band = lax.axis_index("slab"), lax.axis_index("xy")
    first = copy_all([(block_any, block_ref), (cells_any, cells_ref), (vol_any, vol_ref)], small)
    for copy in first:
        copy.start()
    for flip, part in enumerate(parts):
        source = band ^ flip
        piece = part[...].astype(jnp.float32).reshape(views, plan.chunk, plan.unit, tdet)
        halo = jnp.where(
            source == 0,
            0,
            jnp.where(source == plan.bands - 1, plan.units - plan.halo_units, plan.units),
        )
        for v in range(views):
            for i in range(plan.own_units):
                corr[v, plan.halo_units + source * plan.own_units + i] = piece[v, i]
            for i in range(plan.halo_units):
                corr[v, halo + i] = piece[v, plan.own_units + i]
    top = lax.broadcasted_iota(jnp.int32, (8, tdet), 0) == 0
    lane = lax.broadcasted_iota(jnp.int32, (8, tdet), 1)
    for copy in first:
        copy.wait()
    gap_sum = jnp.zeros((rows, tvox), jnp.float32)
    for p in range(planes):
        for t in range(tiles):
            for r in range(rows):
                both = 0.0
                for v in range(views):
                    unit, column = unit_of(plan, block_ref[p, t, v, r], slab)
                    picked = jnp.broadcast_to(corr[v, unit, pl.ds(column, 1), :], (8, tdet))
                    left = jnp.where(top, picked, 1.0)
                    left = jnp.where(lane < cells_ref[p, t, v, r], left, 0.0).astype(jnp.bfloat16)
                    both += lax.dot_general(
                        left,
                        foot[p, r, t, v],
                        (((1,), (1,)), ((), ())),
                        preferred_element_type=jnp.float32,
                    )
                sums[0, r : r + 1] = both[0:1]
                sums[1, r : r + 1] = both[1:2]
            volume = vol_ref[p, :, t * tvox : (t + 1) * tvox]
            sart = jnp.maximum(volume + RELAX * (sums[0] / sums[1]), 0.0)
            out_ref[p * tiles + t] = sart
            gap = sart - volume
            gap_sum += gap * gap
    out_ref[planes * tiles] = gap_sum


def back_project(plan, volume, footprint, tile_block, tile_cells, parts):
    shape = footprint.shape
    planes, rows, tiles, views, tvox, tdet = shape
    spaces = [pl.ANY, pltpu.VMEM, pl.ANY, pl.ANY] + [pltpu.VMEM] * len(parts)
    footprint = pltpu.with_memory_space_constraint(footprint, pltpu.VMEM)
    return pl.pallas_call(
        functools.partial(back_kernel, plan, shape),
        out_shape=jax.ShapeDtypeStruct((planes * tiles + 1, rows, tvox), jnp.float32),
        in_specs=[pl.BlockSpec(memory_space=space) for space in spaces],
        out_specs=pl.BlockSpec(memory_space=pltpu.VMEM),
        scratch_shapes=[
            pltpu.VMEM((2, rows, tvox), jnp.float32),
            pltpu.VMEM((views, plan.units + plan.halo_units, plan.unit, tdet), jnp.float32),
            pltpu.VMEM(volume.shape, jnp.float32),
            pltpu.SMEM(tile_block.shape, jnp.int32),
            pltpu.SMEM(tile_cells.shape, jnp.int32),
            pltpu.SemaphoreType.DMA((3,)),
        ],
        compiler_params=pltpu.CompilerParams(vmem_limit_bytes=VMEM_BYTES // 2),
        name="back_project",
    )(volume, footprint, tile_block, tile_cells, *parts)


def unit_at_edge(cells):
    return cells * lax.rsqrt(cells * cells + SMOOTHING)


def slope_of(here, after, unit_before, first_row, last_row, first_cell, last_cell):
    rows, cells = here.shape
    diff_a = after - here
    diff_b = jnp.where(last_row, 0.0, pltpu.roll(here, rows - 1, 0)) - here
    diff_e = jnp.where(last_cell, 0.0, pltpu.roll(here, cells - 1, 1)) - here
    scale = lax.rsqrt(diff_a * diff_a + diff_b * diff_b + diff_e * diff_e + SMOOTHING)
    unit_a, unit_b, unit_e = diff_a * scale, diff_b * scale, diff_e * scale
    edge = unit_at_edge(here)
    back_b = jnp.where(first_row, edge, pltpu.roll(unit_b, 1, 0))
    back_e = jnp.where(first_cell, edge, pltpu.roll(unit_e, 1, 1))
    return unit_before + back_b + back_e - (unit_a + unit_b + unit_e), unit_a


def smooth_kernel(sizes, near_ref, far_ref, out_ref, field, slopes):
    slabs, bands, planes, rows, tiles, tvox = sizes
    slab, band = lax.axis_index("slab"), lax.axis_index("xy")
    depth, height, width = slabs * planes, bands * rows, tiles * tvox

    gap = jnp.zeros((rows, tvox), jnp.float32)
    for half, ref in enumerate((near_ref, far_ref)):
        for i in range(slabs // 2):
            for j in range(bands):
                plane = (slab ^ (2 * i + half)) * planes
                row = pl.multiple_of((band ^ j) * rows, rows)
                for p in range(planes):
                    for t in range(tiles):
                        field[plane + p, pl.ds(row, rows), t * tvox : (t + 1) * tvox] = ref[
                            i, j, p * tiles + t
                        ]
                gap += ref[i, j, planes * tiles]
    nothing = jnp.zeros((height, width), jnp.float32)
    field[depth] = nothing
    slopes[depth] = nothing
    row_ids = lax.broadcasted_iota(jnp.int32, (height, width), 0)
    cell_ids = lax.broadcasted_iota(jnp.int32, (height, width), 1)
    rims = (row_ids == 0, row_ids == height - 1, cell_ids == 0, cell_ids == width - 1)

    def total(square):
        return jnp.sum(jnp.sum(square, axis=0, keepdims=True), axis=1, keepdims=True)

    def fold(square):
        return jnp.sum(
            sum(square[:, t * tvox : (t + 1) * tvox] for t in range(tiles)).reshape(
                height // 8, 8, tvox
            ),
            axis=0,
        )

    norm = jnp.sqrt(total(gap))

    def one(p, carry):
        unit_before, square = carry
        slope, unit = slope_of(field[p], field[p + 1], unit_before, *rims)
        slopes[p] = slope
        return unit, square + fold(slope * slope)

    start = unit_at_edge(field[0]), jnp.zeros((8, tvox), jnp.float32)
    _, square = lax.fori_loop(0, depth, one, start)
    step = TV_RATE * norm / jnp.sqrt(total(square) + 1e-06)

    def two(p, carry):
        unit_before, here, square = carry
        after = field[p + 1] - step * slopes[p + 1]
        slope, unit = slope_of(here, after, unit_before, *rims)
        field[p] = here
        slopes[p] = slope
        return unit, after, square + fold(slope * slope)

    here = field[0] - step * slopes[0]
    start = unit_at_edge(here), here, jnp.zeros((8, tvox), jnp.float32)
    _, _, square = lax.fori_loop(0, depth, two, start)
    step = TV_RATE * norm / jnp.sqrt(total(square) + 1e-06)
    mine = pl.ds(pl.multiple_of(band * rows, rows), rows)
    for p in range(planes):
        out_ref[p] = field[slab * planes + p, mine, :] - step * slopes[slab * planes + p, mine, :]


def smooth(volume, near, far, slabs, bands, tiles):
    planes, rows, cells = volume.shape
    sizes = slabs, bands, planes, rows, tiles, cells // tiles
    whole = (slabs * planes + 1, bands * rows, cells)
    return pl.pallas_call(
        functools.partial(smooth_kernel, sizes),
        out_shape=jax.ShapeDtypeStruct(volume.shape, jnp.float32),
        in_specs=[pl.BlockSpec(memory_space=pltpu.VMEM)] * 2,
        out_specs=pl.BlockSpec(memory_space=pltpu.VMEM),
        scratch_shapes=[pltpu.VMEM(whole, jnp.float32)] * 2,
        compiler_params=pltpu.CompilerParams(vmem_limit_bytes=VMEM_BYTES),
        name="smooth",
    )(near, far)


def body(volume, footprint, tile_block, tile_cells, measured):
    views, tdet = footprint.shape[3], footprint.shape[5]
    slabs, bands = lax.axis_size("slab"), lax.axis_size("xy")
    plan = Plan(slabs, bands, views, measured.shape[1] // tdet, tdet)
    block, cells = (jnp.transpose(each, (0, 2, 3, 1)) for each in (tile_block, tile_cells))

    packed, low, high, seen, footprint = project(
        plan, volume, footprint, block, cells, measured
    )
    below, above = shift_all(high, "slab", 1), shift_all(low, "slab", -1)
    chunks = shares(plan, packed, below, above)
    parts = [chunks[0]] + [swap_all(chunks[flip], "xy", flip) for flip in range(1, bands)]
    correction, rounded = correct(plan, seen, parts)
    parts = [rounded] + [swap_all(rounded, "xy", flip) for flip in range(1, bands)]
    tiled = back_project(plan, volume, footprint, block, cells, parts)

    line = jnp.stack([tiled] + [swap_all(tiled, "xy", flip) for flip in range(1, bands)])
    near = jnp.stack([line] + [swap_all(line, "slab", flip) for flip in range(2, slabs, 2)])
    far = swap_all(near, "slab", 1)
    updated = smooth(volume, near, far, slabs, bands, footprint.shape[2])
    return (updated, correction)


def solution(mesh):
    placed = (
        P("slab", "xy", None),
        P("slab", "xy", None, None, None, None),
        P("slab", "xy", None, None),
        P("slab", "xy", None, None),
        P(),
    )
    return jax.shard_map(
        body,
        mesh=mesh,
        in_specs=placed,
        out_specs=(P("slab", "xy", None), P(None, ("slab", "xy"))),
        check_vma=False,
    )
```

```python
import functools

import jax
import jax.numpy as jnp
from jax import lax
from jax.experimental import pallas as pl
from jax.experimental.pallas import tpu as pltpu
from jax.sharding import PartitionSpec as P

RELAX = 1.0
TV_RATE = 0.8
SMOOTHING = 0.01
DCOLS = 2048
VMEM_BYTES = 32 * 1024 * 1024


class Plan:
    def __init__(self, slabs, bands, views, nblocks, tdet):
        self.slabs, self.bands, self.views, self.tdet = slabs, bands, views, tdet
        per_row = DCOLS // tdet
        own = nblocks // (slabs * bands)
        self.slab_own = nblocks // slabs
        self.halo = per_row
        self.unit = min(per_row, own)
        self.own_units = own // self.unit
        self.halo_units = per_row // self.unit
        self.units = self.slab_own // self.unit + 2 * self.halo_units
        self.chunk = self.own_units + self.halo_units
        narrow = per_row // bands
        fits = self.unit == per_row and narrow * bands == per_row and narrow + 2 < per_row
        self.narrow = narrow if fits else 0
        self.width = [
            self.narrow + 2 if v % 2 and self.narrow else self.unit for v in range(views)
        ]
        self.base = [2 * sum(self.width[:v]) for v in range(views)]
        self.lines = 2 * sum(self.width)

    def is_narrow(self, v):
        return self.width[v] != self.unit


def shift_all(cells, axis, step):
    count = lax.axis_size(axis)
    return lax.ppermute(cells, axis, [(i, (i + step) % count) for i in range(count)])


def swap_all(cells, axis, flip):
    count = lax.axis_size(axis)
    return lax.ppermute(cells, axis, [(i, i ^ flip) for i in range(count)])


def unit_of(plan, block, slab):
    local = jnp.clip(
        block - slab * plan.slab_own + plan.halo, 0, plan.units * plan.unit - 1
    )
    return lax.div(local, plan.unit), lax.rem(local, plan.unit)


def copy_all(pairs, sems):
    return [pltpu.make_async_copy(src, dst, sems.at[n]) for n, (src, dst) in enumerate(pairs)]


def project_kernel(
    plan, shape, vol_hbm, foot_hbm, block_hbm, cells_hbm, seen_hbm,
    out_ref, low_ref, high_ref, seen_ref, foot, acc, vol_ref, block_ref, cells_ref, seen, sems, small,
):
    planes, rows, tiles, views, tvox, tdet = shape
    slab, band = lax.axis_index("slab"), lax.axis_index("xy")
    parts = sems.shape[0]
    step = planes * rows // parts
    spans = [(n * step // rows, pl.ds(n * step % rows, step)) for n in range(parts)]
    span = plan.unit * tdet
    own_at = (slab * plan.bands + band) * plan.own_units
    halo_at = jnp.where(
        band == 0,
        slab * (plan.slab_own // plan.unit) - plan.halo_units,
        (slab + 1) * (plan.slab_own // plan.unit),
    )
    halo_at = jnp.clip(halo_at, 0, seen_hbm.shape[1] // span - plan.halo_units)
    own_at, halo_at = (pl.multiple_of(at * span, span) for at in (own_at, halo_at))
    own_size, halo_size = plan.own_units * span, plan.halo_units * span
    first = copy_all(
        [
            (block_hbm, block_ref),
            (cells_hbm, cells_ref),
            (vol_hbm, vol_ref),
            (seen_hbm.at[:, pl.ds(own_at, own_size)], seen.at[:, pl.ds(0, own_size)]),
            (seen_hbm.at[:, pl.ds(halo_at, halo_size)], seen.at[:, pl.ds(own_size, halo_size)]),
        ],
        small,
    )
    stream = copy_all([(foot_hbm.at[p, at], foot.at[p, at]) for p, at in spans], sems)
    for copy in first + stream:
        copy.start()
    acc[...] = jnp.zeros_like(acc)
    top = lax.broadcasted_iota(jnp.int32, (8, tvox), 0) == 0
    lane = lax.broadcasted_iota(jnp.int32, (8, tdet), 1)
    for copy in first:
        copy.wait()
    for v in range(views):
        for i in range(plan.chunk):
            for c in range(plan.unit):
                at = (i * plan.unit + c) * tdet
                seen_ref[v, i, c : c + 1, :] = seen[v : v + 1, at : at + tdet]
    starts = [plan.units * sum(plan.width[:v]) for v in range(views)]
    for n in range(parts):
        stream[n].wait()
        for p, r in [divmod(n * step + k, rows) for k in range(step)]:
            for t in range(tiles):
                voxels = vol_ref[p, r : r + 1, t * tvox : (t + 1) * tvox]
                left = jnp.where(top, jnp.broadcast_to(voxels, (8, tvox)), 1.0)
                left = left.astype(jnp.bfloat16)
                for v in range(views):
                    sums = jnp.dot(left, foot[p, r, t, v], preferred_element_type=jnp.float32)
                    sums = jnp.where(lane < cells_ref[p, t, v, r], sums, 0.0)
                    unit, column = unit_of(plan, block_ref[p, t, v, r], slab)
                    if plan.is_narrow(v):
                        column = column - (band * plan.narrow - 1)
                        column = jnp.clip(column, 0, plan.width[v] - 1)
                    acc[starts[v] + unit * plan.width[v] + column] += sums
    for unit in range(plan.units):
        for v in range(views):
            width = plan.width[v]
            at = starts[v] + unit * width
            for q in range(2):
                line = plan.base[v] + q * width
                out_ref[unit, line : line + width, :] = acc[at : at + width, q, :]
    edge = 2 * plan.halo_units
    low_ref[...] = out_ref[:edge]
    high_ref[...] = out_ref[plan.units - edge :]


def in_vmem(count):
    return [pl.BlockSpec(memory_space=pltpu.VMEM)] * count


def project(plan, volume, footprint, tile_block, tile_cells, measured):
    shape = footprint.shape
    planes, rows = shape[:2]
    views, tdet = plan.views, plan.tdet
    parts = 2 * planes if rows % 2 == 0 else planes
    operands = [
        pltpu.with_memory_space_constraint(operand, pltpu.HBM)
        for operand in (volume, footprint, tile_block, tile_cells, measured)
    ]
    border = (2 * plan.halo_units, plan.lines, tdet)
    return pl.pallas_call(
        functools.partial(project_kernel, plan, shape),
        out_shape=(
            jax.ShapeDtypeStruct((plan.units, plan.lines, tdet), jnp.float32),
            jax.ShapeDtypeStruct(border, jnp.float32),
            jax.ShapeDtypeStruct(border, jnp.float32),
            jax.ShapeDtypeStruct((views, plan.chunk, plan.unit, tdet), jnp.float32),
            pltpu.VMEM(shape, jnp.bfloat16),
        ),
        in_specs=[pl.BlockSpec(memory_space=pltpu.HBM)] * 5,
        out_specs=tuple(in_vmem(5)),
        scratch_shapes=[
            pltpu.VMEM((plan.units * sum(plan.width), 8, tdet), jnp.float32),
            pltpu.VMEM(volume.shape, jnp.float32),
            pltpu.SMEM(tile_block.shape, jnp.int32),
            pltpu.SMEM(tile_cells.shape, jnp.int32),
            pltpu.VMEM((views, plan.chunk * plan.unit * tdet), jnp.float32),
            pltpu.SemaphoreType.DMA((parts,)),
            pltpu.SemaphoreType.DMA((5,)),
        ],
        compiler_params=pltpu.CompilerParams(vmem_limit_bytes=VMEM_BYTES),
        name="project",
    )(*operands)


def share_kernel(plan, packed_ref, below_ref, above_ref, *rest):
    out_refs, total = rest[:-1], rest[-1]
    slab, band = lax.axis_index("slab"), lax.axis_index("xy")
    edge = 2 * plan.halo_units
    total[...] = packed_ref[...]
    total[:edge] += jnp.where(slab == 0, 0.0, below_ref[...])
    total[plan.units - edge :] += jnp.where(slab == plan.slabs - 1, 0.0, above_ref[...])
    for flip, out_ref in enumerate(out_refs):
        owner = band ^ flip
        for i in range(plan.own_units):
            out_ref[i] = total[plan.halo_units + owner * plan.own_units + i]
        halo = jnp.where(owner == 0, 0, plan.units - plan.halo_units)
        for i in range(plan.halo_units):
            out_ref[plan.own_units + i] = total[halo + i]


def shares(plan, packed, below, above):
    chunk = jax.ShapeDtypeStruct((plan.chunk,) + packed.shape[1:], jnp.float32)
    return pl.pallas_call(
        functools.partial(share_kernel, plan),
        out_shape=(chunk,) * plan.bands,
        in_specs=in_vmem(3),
        out_specs=tuple(in_vmem(plan.bands)),
        scratch_shapes=[pltpu.VMEM(packed.shape, jnp.float32)],
        compiler_params=pltpu.CompilerParams(vmem_limit_bytes=VMEM_BYTES // 4),
        name="shares",
    )(packed, below, above)


def correct_kernel(plan, seen_ref, *rest):
    parts, (exact_ref, rounded_ref) = rest[:-2], rest[-2:]
    band = lax.axis_index("xy")
    tdet, unit = plan.tdet, plan.unit
    rounded = []
    for v in range(plan.views):
        width = plan.width[v]
        for i in range(plan.chunk):
            sums = []
            for q in range(2):
                line = plan.base[v] + q * width
                total = 0.0
                for flip, part in enumerate(parts):
                    piece = part[i, line : line + width, :]
                    if plan.is_narrow(v):
                        room = jnp.zeros((unit - width, tdet), jnp.float32)
                        piece = jnp.concatenate([piece, room], axis=0)
                        first = (band ^ flip) * plan.narrow - 1
                        piece = pltpu.roll(piece, lax.rem(first + unit, unit), 0)
                    total = total + piece
                sums.append(total)
            corrected = (seen_ref[v, i] - sums[0]) / jnp.maximum(sums[1], 1.0)
            rounded.append(corrected)
            if i < plan.own_units:
                exact_ref[v, i] = corrected
    rounded_ref[...] = jnp.concatenate(rounded, axis=0).astype(jnp.bfloat16)


def correct(plan, seen, parts):
    views, chunk, unit, tdet = seen.shape
    return pl.pallas_call(
        functools.partial(correct_kernel, plan),
        out_shape=(
            jax.ShapeDtypeStruct((views, plan.own_units, unit, tdet), jnp.float32),
            jax.ShapeDtypeStruct((views * chunk * unit, tdet), jnp.bfloat16),
        ),
        in_specs=in_vmem(1 + len(parts)),
        out_specs=tuple(in_vmem(2)),
        compiler_params=pltpu.CompilerParams(vmem_limit_bytes=VMEM_BYTES // 4),
        name="correct",
    )(seen, *parts)


def back_kernel(plan, shape, vol_any, foot, block_any, cells_any, *rest):
    parts, (out_ref, sums, corr, vol_ref, block_ref, cells_ref, small) = rest[:-7], rest[-7:]
    planes, rows, tiles, views, tvox, tdet = shape
    slab, band = lax.axis_index("slab"), lax.axis_index("xy")
    first = copy_all([(block_any, block_ref), (cells_any, cells_ref), (vol_any, vol_ref)], small)
    for copy in first:
        copy.start()
    for flip, part in enumerate(parts):
        source = band ^ flip
        piece = part[...].astype(jnp.float32).reshape(views, plan.chunk, plan.unit, tdet)
        halo = jnp.where(
            source == 0,
            0,
            jnp.where(source == plan.bands - 1, plan.units - plan.halo_units, plan.units),
        )
        for v in range(views):
            for i in range(plan.own_units):
                corr[v, plan.halo_units + source * plan.own_units + i] = piece[v, i]
            for i in range(plan.halo_units):
                corr[v, halo + i] = piece[v, plan.own_units + i]
    top = lax.broadcasted_iota(jnp.int32, (8, tdet), 0) == 0
    lane = lax.broadcasted_iota(jnp.int32, (8, tdet), 1)
    for copy in first:
        copy.wait()
    gap_sum = jnp.zeros((rows, tvox), jnp.float32)
    for p in range(planes):
        for t in range(tiles):
            for r in range(rows):
                both = 0.0
                for v in range(views):
                    unit, column = unit_of(plan, block_ref[p, t, v, r], slab)
                    picked = jnp.broadcast_to(corr[v, unit, pl.ds(column, 1), :], (8, tdet))
                    left = jnp.where(top, picked, 1.0)
                    left = jnp.where(lane < cells_ref[p, t, v, r], left, 0.0).astype(jnp.bfloat16)
                    both += lax.dot_general(
                        left,
                        foot[p, r, t, v],
                        (((1,), (1,)), ((), ())),
                        preferred_element_type=jnp.float32,
                    )
                sums[0, r : r + 1] = both[0:1]
                sums[1, r : r + 1] = both[1:2]
            volume = vol_ref[p, :, t * tvox : (t + 1) * tvox]
            sart = jnp.maximum(volume + RELAX * (sums[0] / sums[1]), 0.0)
            out_ref[p * tiles + t] = sart
            gap = sart - volume
            gap_sum += gap * gap
    out_ref[planes * tiles] = gap_sum


def back_project(plan, volume, footprint, tile_block, tile_cells, parts):
    shape = footprint.shape
    planes, rows, tiles, views, tvox, tdet = shape
    spaces = [pl.ANY, pltpu.VMEM, pl.ANY, pl.ANY] + [pltpu.VMEM] * len(parts)
    footprint = pltpu.with_memory_space_constraint(footprint, pltpu.VMEM)
    return pl.pallas_call(
        functools.partial(back_kernel, plan, shape),
        out_shape=jax.ShapeDtypeStruct((planes * tiles + 1, rows, tvox), jnp.float32),
        in_specs=[pl.BlockSpec(memory_space=space) for space in spaces],
        out_specs=pl.BlockSpec(memory_space=pltpu.VMEM),
        scratch_shapes=[
            pltpu.VMEM((2, rows, tvox), jnp.float32),
            pltpu.VMEM((views, plan.units + plan.halo_units, plan.unit, tdet), jnp.float32),
            pltpu.VMEM(volume.shape, jnp.float32),
            pltpu.SMEM(tile_block.shape, jnp.int32),
            pltpu.SMEM(tile_cells.shape, jnp.int32),
            pltpu.SemaphoreType.DMA((3,)),
        ],
        compiler_params=pltpu.CompilerParams(vmem_limit_bytes=VMEM_BYTES // 2),
        name="back_project",
    )(volume, footprint, tile_block, tile_cells, *parts)


def unit_at_rim(cells):
    return cells * lax.rsqrt(cells * cells + SMOOTHING)


def slope_of(here, after, unit_before, size, masks):
    high, wide = size
    first_row, last_row, first_cell, last_cell = masks
    lanes = here[0, 0].shape[1]
    next_row = {k: pltpu.roll(x, 7, 0) for k, x in here.items()}
    next_cell = {k: pltpu.roll(x, lanes - 1, 1) for k, x in here.items()}
    slope, unit_a, unit_b, unit_e = {}, {}, {}, {}
    for i, t in here:
        k, x = (i, t), here[i, t]
        row = next_row[i + 1, t] if i + 1 < high else 0.0
        cell = next_cell[i, t + 1] if t + 1 < wide else 0.0
        diff_a = after[k] - x
        diff_b = jnp.where(last_row, row, next_row[k]) - x
        diff_e = jnp.where(last_cell, cell, next_cell[k]) - x
        scale = lax.rsqrt(diff_a * diff_a + diff_b * diff_b + diff_e * diff_e + SMOOTHING)
        unit_a[k], unit_b[k], unit_e[k] = diff_a * scale, diff_b * scale, diff_e * scale
        slope[k] = unit_before[k] - (diff_a + diff_b + diff_e) * scale
    past_row = {k: pltpu.roll(x, 1, 0) for k, x in unit_b.items()}
    past_cell = {k: pltpu.roll(x, 1, 1) for k, x in unit_e.items()}
    for i, t in here:
        k = (i, t)
        rim = unit_at_rim(here[k]) if i == 0 or t == 0 else None
        row = past_row[i - 1, t] if i else rim
        cell = past_cell[i, t - 1] if t else rim
        slope[k] += jnp.where(first_row, row, past_row[k])
        slope[k] += jnp.where(first_cell, cell, past_cell[k])
    return slope, unit_a


def smooth_kernel(sizes, near_ref, far_ref, exact_ref, out_ref, seen_ref, field, slopes, units):
    slabs, bands, planes, rows, tiles, tvox = sizes
    slab, band = lax.axis_index("slab"), lax.axis_index("xy")
    depth, per = slabs * planes, rows // 8
    size = bands * per, tiles
    blocks = [(i, t) for i in range(size[0]) for t in range(size[1])]

    views, own, unit, tdet = exact_ref.shape
    for v in range(views):
        for i in range(own):
            for c in range(unit):
                at = (i * unit + c) * tdet
                seen_ref[v : v + 1, at : at + tdet] = exact_ref[v, i, c : c + 1, :]

    gap = jnp.zeros((rows, tvox), jnp.float32)
    for half, ref in enumerate((near_ref, far_ref)):
        for i in range(slabs // 2):
            for j in range(bands):
                plane, at = (slab ^ (2 * i + half)) * planes, (band ^ j) * per
                for p in range(planes):
                    for t in range(tiles):
                        tile = ref[i, j, p * tiles + t]
                        for n in range(per):
                            field[plane + p, at + n, t] = tile[8 * n : 8 * n + 8]
                gap += ref[i, j, planes * tiles]
    nothing = jnp.zeros((8, tvox), jnp.float32)
    for i, t in blocks:
        field[depth, i, t] = nothing
        slopes[depth, i, t] = nothing
    row_ids = lax.broadcasted_iota(jnp.int32, (8, tvox), 0)
    cell_ids = lax.broadcasted_iota(jnp.int32, (8, tvox), 1)
    masks = (row_ids == 0, row_ids == 7, cell_ids == 0, cell_ids == tvox - 1)

    def total(square):
        return jnp.sum(jnp.sum(square, axis=0, keepdims=True), axis=1, keepdims=True)

    def finish(p, here, after, square):
        before = {(i, t): units[i, t] for i, t in blocks}
        slope, unit_a = slope_of(here, after, before, size, masks)
        for i, t in blocks:
            slopes[p, i, t] = slope[i, t]
            units[i, t] = unit_a[i, t]
            square = square + slope[i, t] * slope[i, t]
        return square

    norm = jnp.sqrt(total(gap))
    unroll = 4 if depth % 4 == 0 and len(blocks) <= 16 else 1

    def one(p, square):
        here = {(i, t): field[p, i, t] for i, t in blocks}
        after = {(i, t): field[p + 1, i, t] for i, t in blocks}
        return finish(p, here, after, square)

    for i, t in blocks:
        units[i, t] = unit_at_rim(field[0, i, t])
    square = lax.fori_loop(0, depth, one, nothing, unroll=unroll)
    step = TV_RATE * norm / jnp.sqrt(total(square) + 1e-06)

    def two(p, square):
        here = {(i, t): field[p, i, t] for i, t in blocks}
        after = {(i, t): field[p + 1, i, t] - step * slopes[p + 1, i, t] for i, t in blocks}
        for i, t in blocks:
            field[p + 1, i, t] = after[i, t]
        return finish(p, here, after, square)

    for i, t in blocks:
        here = field[0, i, t] - step * slopes[0, i, t]
        field[0, i, t] = here
        units[i, t] = unit_at_rim(here)
    square = lax.fori_loop(0, depth, two, nothing, unroll=unroll)
    step = TV_RATE * norm / jnp.sqrt(total(square) + 1e-06)
    for p in range(planes):
        for n in range(per):
            for t in range(tiles):
                at = slab * planes + p, band * per + n, t
                out_ref[p, 8 * n : 8 * n + 8, t * tvox : (t + 1) * tvox] = (
                    field[at] - step * slopes[at]
                )


def smooth(volume, near, far, exact, slabs, bands, tiles):
    planes, rows, cells = volume.shape
    views, own, unit, tdet = exact.shape
    sizes = slabs, bands, planes, rows, tiles, cells // tiles
    plane = bands * rows // 8, tiles, 8, cells // tiles
    return pl.pallas_call(
        functools.partial(smooth_kernel, sizes),
        out_shape=(
            jax.ShapeDtypeStruct(volume.shape, jnp.float32),
            jax.ShapeDtypeStruct((views, own * unit * tdet), jnp.float32),
        ),
        in_specs=in_vmem(3),
        out_specs=tuple(in_vmem(2)),
        scratch_shapes=[
            pltpu.VMEM((slabs * planes + 1,) + plane, jnp.float32),
            pltpu.VMEM((slabs * planes + 1,) + plane, jnp.float32),
            pltpu.VMEM(plane, jnp.float32),
        ],
        compiler_params=pltpu.CompilerParams(vmem_limit_bytes=VMEM_BYTES),
        name="smooth",
    )(near, far, exact)


def body(volume, footprint, tile_block, tile_cells, measured):
    views, tdet = footprint.shape[3], footprint.shape[5]
    slabs, bands = lax.axis_size("slab"), lax.axis_size("xy")
    plan = Plan(slabs, bands, views, measured.shape[1] // tdet, tdet)
    block, cells = (jnp.transpose(each, (0, 2, 3, 1)) for each in (tile_block, tile_cells))

    packed, low, high, seen, footprint = project(
        plan, volume, footprint, block, cells, measured
    )
    below, above = shift_all(high, "slab", 1), shift_all(low, "slab", -1)
    chunks = shares(plan, packed, below, above)
    parts = [chunks[0]] + [swap_all(chunks[flip], "xy", flip) for flip in range(1, bands)]
    exact, rounded = correct(plan, seen, parts)
    parts = [rounded] + [swap_all(rounded, "xy", flip) for flip in range(1, bands)]
    tiled = back_project(plan, volume, footprint, block, cells, parts)

    line = jnp.stack([tiled] + [swap_all(tiled, "xy", flip) for flip in range(1, bands)])
    near = jnp.stack([line] + [swap_all(line, "slab", flip) for flip in range(2, slabs, 2)])
    far = swap_all(near, "slab", 1)
    return smooth(volume, near, far, exact, slabs, bands, footprint.shape[2])


def solution(mesh):
    placed = (
        P("slab", "xy", None),
        P("slab", "xy", None, None, None, None),
        P("slab", "xy", None, None),
        P("slab", "xy", None, None),
        P(),
    )
    return jax.shard_map(
        body,
        mesh=mesh,
        in_specs=placed,
        out_specs=(P("slab", "xy", None), P(None, ("slab", "xy"))),
        check_vma=False,
    )
```

```python
import functools

import jax
import jax.numpy as jnp
from jax import lax
from jax.experimental import pallas as pl
from jax.experimental.pallas import tpu as pltpu
from jax.sharding import PartitionSpec as P

RELAX = 1.0
TV_RATE = 0.8
SMOOTHING = 0.01
DCOLS = 2048
VMEM_BYTES = 32 * 1024 * 1024


class Plan:
    def __init__(self, slabs, bands, views, nblocks, tdet):
        self.slabs, self.bands, self.views, self.tdet = slabs, bands, views, tdet
        per_row = DCOLS // tdet
        own = nblocks // (slabs * bands)
        self.slab_own = nblocks // slabs
        self.halo = per_row
        self.unit = min(per_row, own)
        self.own_units = own // self.unit
        self.halo_units = per_row // self.unit
        self.units = self.slab_own // self.unit + 2 * self.halo_units
        self.chunk = self.own_units + self.halo_units
        narrow = per_row // bands
        fits = self.unit == per_row and narrow * bands == per_row and narrow + 2 < per_row
        self.narrow = narrow if fits else 0
        self.width = [
            self.narrow + 2 if v % 2 and self.narrow else self.unit for v in range(views)
        ]
        self.base = [2 * sum(self.width[:v]) for v in range(views)]
        self.lines = 2 * sum(self.width)

    def is_narrow(self, v):
        return self.width[v] != self.unit


def shift_all(cells, axis, step):
    count = lax.axis_size(axis)
    return lax.ppermute(cells, axis, [(i, (i + step) % count) for i in range(count)])


def reduce_order(bands):
    return [0] + [flip for flip in (3, 1, 2) if flip < bands] + list(range(4, bands))


def swap_all(cells, axis, flip):
    count = lax.axis_size(axis)
    return lax.ppermute(cells, axis, [(i, i ^ flip) for i in range(count)])


def unit_of(plan, block, slab):
    local = jnp.clip(
        block - slab * plan.slab_own + plan.halo, 0, plan.units * plan.unit - 1
    )
    return lax.div(local, plan.unit), lax.rem(local, plan.unit)


def copy_all(pairs, sems):
    return [pltpu.make_async_copy(src, dst, sems.at[n]) for n, (src, dst) in enumerate(pairs)]


def stream_spans(planes, rows):
    size = max(rows // 4, 1)
    return [(p, r, min(size, rows - r)) for p in range(planes) for r in range(0, rows, size)]


def project_kernel(
    plan, shape, vol_hbm, foot_hbm, block_hbm, cells_hbm, seen_hbm,
    out_ref, low_ref, high_ref, seen_ref, foot, acc, vol_ref, block_ref, cells_ref, seen, sems, small,
):
    planes, rows, tiles, views, tvox, tdet = shape
    slab, band = lax.axis_index("slab"), lax.axis_index("xy")
    spans = stream_spans(planes, rows)
    span = plan.unit * tdet
    own_at = (slab * plan.bands + band) * plan.own_units
    halo_at = jnp.where(
        band == 0,
        slab * (plan.slab_own // plan.unit) - plan.halo_units,
        (slab + 1) * (plan.slab_own // plan.unit),
    )
    halo_at = jnp.clip(halo_at, 0, seen_hbm.shape[1] // span - plan.halo_units)
    own_at, halo_at = (pl.multiple_of(at * span, span) for at in (own_at, halo_at))
    own_size, halo_size = plan.own_units * span, plan.halo_units * span
    first = copy_all(
        [
            (block_hbm, block_ref),
            (cells_hbm, cells_ref),
            (vol_hbm, vol_ref),
            (seen_hbm.at[:, pl.ds(own_at, own_size)], seen.at[:, pl.ds(0, own_size)]),
            (seen_hbm.at[:, pl.ds(halo_at, halo_size)], seen.at[:, pl.ds(own_size, halo_size)]),
        ],
        small,
    )
    stream = [(foot_hbm.at[p, pl.ds(r, n)], foot.at[p, pl.ds(r, n)]) for p, r, n in spans]
    stream = copy_all(stream, sems)
    for copy in first:
        copy.start()
    for copy in stream:
        copy.start(priority=1)
    acc[...] = jnp.zeros_like(acc)
    top = lax.broadcasted_iota(jnp.int32, (8, tvox), 0) == 0
    lane = lax.broadcasted_iota(jnp.int32, (8, tdet), 1)
    for copy in first:
        copy.wait()
    for v in range(views):
        for i in range(plan.chunk):
            for c in range(plan.unit):
                at = (i * plan.unit + c) * tdet
                seen_ref[v, i, c : c + 1, :] = seen[v : v + 1, at : at + tdet]
    starts = [plan.units * sum(plan.width[:v]) for v in range(views)]
    for copy, (p, begin, size) in zip(stream, spans):
        copy.wait()
        for r in range(begin, begin + size):
            for t in range(tiles):
                voxels = vol_ref[p, r : r + 1, t * tvox : (t + 1) * tvox]
                left = jnp.where(top, jnp.broadcast_to(voxels, (8, tvox)), 1.0)
                left = left.astype(jnp.bfloat16)
                for v in range(views):
                    sums = jnp.dot(left, foot[p, r, t, v], preferred_element_type=jnp.float32)
                    sums = jnp.where(lane < cells_ref[p, t, v, r], sums, 0.0)
                    unit, column = unit_of(plan, block_ref[p, t, v, r], slab)
                    if plan.is_narrow(v):
                        column = column - (band * plan.narrow - 1)
                        column = jnp.clip(column, 0, plan.width[v] - 1)
                    acc[starts[v] + unit * plan.width[v] + column] += sums
    for unit in range(plan.units):
        for v in range(views):
            width = plan.width[v]
            at = starts[v] + unit * width
            for q in range(2):
                line = plan.base[v] + q * width
                out_ref[unit, line : line + width, :] = acc[at : at + width, q, :]
    edge = 2 * plan.halo_units
    low_ref[...] = out_ref[:edge]
    high_ref[...] = out_ref[plan.units - edge :]


def in_vmem(count):
    return [pl.BlockSpec(memory_space=pltpu.VMEM)] * count


def project(plan, volume, footprint, tile_block, tile_cells, measured):
    shape = footprint.shape
    views, tdet = plan.views, plan.tdet
    parts = len(stream_spans(*shape[:2]))
    operands = [
        pltpu.with_memory_space_constraint(operand, pltpu.HBM)
        for operand in (volume, footprint, tile_block, tile_cells, measured)
    ]
    border = (2 * plan.halo_units, plan.lines, tdet)
    return pl.pallas_call(
        functools.partial(project_kernel, plan, shape),
        out_shape=(
            jax.ShapeDtypeStruct((plan.units, plan.lines, tdet), jnp.float32),
            jax.ShapeDtypeStruct(border, jnp.float32),
            jax.ShapeDtypeStruct(border, jnp.float32),
            jax.ShapeDtypeStruct((views, plan.chunk, plan.unit, tdet), jnp.float32),
            pltpu.VMEM(shape, jnp.bfloat16),
        ),
        in_specs=[pl.BlockSpec(memory_space=pltpu.HBM)] * 5,
        out_specs=tuple(in_vmem(5)),
        scratch_shapes=[
            pltpu.VMEM((plan.units * sum(plan.width), 8, tdet), jnp.float32),
            pltpu.VMEM(volume.shape, jnp.float32),
            pltpu.SMEM(tile_block.shape, jnp.int32),
            pltpu.SMEM(tile_cells.shape, jnp.int32),
            pltpu.VMEM((views, plan.chunk * plan.unit * tdet), jnp.float32),
            pltpu.SemaphoreType.DMA((parts,)),
            pltpu.SemaphoreType.DMA((5,)),
        ],
        compiler_params=pltpu.CompilerParams(vmem_limit_bytes=VMEM_BYTES),
        name="project",
    )(*operands)


def share_kernel(plan, packed_ref, below_ref, above_ref, *rest):
    out_refs, total = rest[:-1], rest[-1]
    slab, band = lax.axis_index("slab"), lax.axis_index("xy")
    edge = 2 * plan.halo_units
    total[...] = packed_ref[...]
    total[:edge] += jnp.where(slab == 0, 0.0, below_ref[...])
    total[plan.units - edge :] += jnp.where(slab == plan.slabs - 1, 0.0, above_ref[...])
    for flip, out_ref in enumerate(out_refs):
        owner = band ^ flip
        for i in range(plan.own_units):
            out_ref[i] = total[plan.halo_units + owner * plan.own_units + i]
        halo = jnp.where(owner == 0, 0, plan.units - plan.halo_units)
        for i in range(plan.halo_units):
            out_ref[plan.own_units + i] = total[halo + i]


def shares(plan, packed, below, above):
    chunk = jax.ShapeDtypeStruct((plan.chunk,) + packed.shape[1:], jnp.float32)
    return pl.pallas_call(
        functools.partial(share_kernel, plan),
        out_shape=(chunk,) * plan.bands,
        in_specs=in_vmem(3),
        out_specs=tuple(in_vmem(plan.bands)),
        scratch_shapes=[pltpu.VMEM(packed.shape, jnp.float32)],
        compiler_params=pltpu.CompilerParams(vmem_limit_bytes=VMEM_BYTES // 4),
        name="shares",
    )(packed, below, above)


def correct_kernel(plan, seen_ref, *rest):
    parts, (exact_ref, rounded_ref) = rest[:-2], rest[-2:]
    band = lax.axis_index("xy")
    tdet, unit = plan.tdet, plan.unit
    rounded = []
    for v in range(plan.views):
        width = plan.width[v]
        for i in range(plan.chunk):
            sums = []
            for q in range(2):
                line = plan.base[v] + q * width
                total = 0.0
                for flip, part in zip(reduce_order(plan.bands), parts):
                    piece = part[i, line : line + width, :]
                    if plan.is_narrow(v):
                        room = jnp.zeros((unit - width, tdet), jnp.float32)
                        piece = jnp.concatenate([piece, room], axis=0)
                        first = (band ^ flip) * plan.narrow - 1
                        piece = pltpu.roll(piece, lax.rem(first + unit, unit), 0)
                    total = total + piece
                sums.append(total)
            corrected = (seen_ref[v, i] - sums[0]) / jnp.maximum(sums[1], 1.0)
            rounded.append(corrected)
            if i < plan.own_units:
                exact_ref[v, i] = corrected
    rounded_ref[...] = jnp.concatenate(rounded, axis=0).astype(jnp.bfloat16)


def correct(plan, seen, parts):
    views, chunk, unit, tdet = seen.shape
    return pl.pallas_call(
        functools.partial(correct_kernel, plan),
        out_shape=(
            jax.ShapeDtypeStruct((views, plan.own_units, unit, tdet), jnp.float32),
            jax.ShapeDtypeStruct((views * chunk * unit, tdet), jnp.bfloat16),
        ),
        in_specs=in_vmem(1 + len(parts)),
        out_specs=tuple(in_vmem(2)),
        compiler_params=pltpu.CompilerParams(vmem_limit_bytes=VMEM_BYTES // 4),
        name="correct",
    )(seen, *parts)


def back_kernel(plan, shape, vol_any, foot, block_any, cells_any, *rest):
    parts, (out_ref, sums, corr, vol_ref, block_ref, cells_ref, small) = rest[:-7], rest[-7:]
    planes, rows, tiles, views, tvox, tdet = shape
    slab, band = lax.axis_index("slab"), lax.axis_index("xy")
    first = copy_all([(block_any, block_ref), (cells_any, cells_ref), (vol_any, vol_ref)], small)
    for copy in first:
        copy.start()
    for flip, part in enumerate(parts):
        source = band ^ flip
        piece = part[...].astype(jnp.float32).reshape(views, plan.chunk, plan.unit, tdet)
        halo = jnp.where(
            source == 0,
            0,
            jnp.where(source == plan.bands - 1, plan.units - plan.halo_units, plan.units),
        )
        for v in range(views):
            for i in range(plan.own_units):
                corr[v, plan.halo_units + source * plan.own_units + i] = piece[v, i]
            for i in range(plan.halo_units):
                corr[v, halo + i] = piece[v, plan.own_units + i]
    top = lax.broadcasted_iota(jnp.int32, (8, tdet), 0) == 0
    lane = lax.broadcasted_iota(jnp.int32, (8, tdet), 1)
    for copy in first:
        copy.wait()
    gap_sum = jnp.zeros((rows, tvox), jnp.float32)
    for p in range(planes):
        for t in range(tiles):
            for r in range(rows):
                both = 0.0
                for v in range(views):
                    unit, column = unit_of(plan, block_ref[p, t, v, r], slab)
                    picked = jnp.broadcast_to(corr[v, unit, pl.ds(column, 1), :], (8, tdet))
                    left = jnp.where(top, picked, 1.0)
                    left = jnp.where(lane < cells_ref[p, t, v, r], left, 0.0).astype(jnp.bfloat16)
                    both += lax.dot_general(
                        left,
                        foot[p, r, t, v],
                        (((1,), (1,)), ((), ())),
                        preferred_element_type=jnp.float32,
                    )
                sums[0, r : r + 1] = both[0:1]
                sums[1, r : r + 1] = both[1:2]
            volume = vol_ref[p, :, t * tvox : (t + 1) * tvox]
            sart = jnp.maximum(volume + RELAX * (sums[0] / sums[1]), 0.0)
            out_ref[p * tiles + t] = sart
            gap = sart - volume
            gap_sum += gap * gap
    out_ref[planes * tiles] = gap_sum


def back_project(plan, volume, footprint, tile_block, tile_cells, parts):
    shape = footprint.shape
    planes, rows, tiles, views, tvox, tdet = shape
    spaces = [pl.ANY, pltpu.VMEM, pl.ANY, pl.ANY] + [pltpu.VMEM] * len(parts)
    footprint = pltpu.with_memory_space_constraint(footprint, pltpu.VMEM)
    return pl.pallas_call(
        functools.partial(back_kernel, plan, shape),
        out_shape=jax.ShapeDtypeStruct((planes * tiles + 1, rows, tvox), jnp.float32),
        in_specs=[pl.BlockSpec(memory_space=space) for space in spaces],
        out_specs=pl.BlockSpec(memory_space=pltpu.VMEM),
        scratch_shapes=[
            pltpu.VMEM((2, rows, tvox), jnp.float32),
            pltpu.VMEM((views, plan.units + plan.halo_units, plan.unit, tdet), jnp.float32),
            pltpu.VMEM(volume.shape, jnp.float32),
            pltpu.SMEM(tile_block.shape, jnp.int32),
            pltpu.SMEM(tile_cells.shape, jnp.int32),
            pltpu.SemaphoreType.DMA((3,)),
        ],
        compiler_params=pltpu.CompilerParams(vmem_limit_bytes=VMEM_BYTES // 2),
        name="back_project",
    )(volume, footprint, tile_block, tile_cells, *parts)


def unit_at_rim(cells):
    return cells * lax.rsqrt(cells * cells + SMOOTHING)


def slope_of(here, after, unit_before, size, masks):
    high, wide = size
    first_row, last_row, first_cell, last_cell = masks
    lanes = here[0, 0].shape[1]
    next_row = {k: pltpu.roll(x, 7, 0) for k, x in here.items()}
    next_cell = {k: pltpu.roll(x, lanes - 1, 1) for k, x in here.items()}
    slope, unit_a, unit_b, unit_e = {}, {}, {}, {}
    for i, t in here:
        k, x = (i, t), here[i, t]
        row = next_row[i + 1, t] if i + 1 < high else 0.0
        cell = next_cell[i, t + 1] if t + 1 < wide else 0.0
        diff_a = after[k] - x
        diff_b = jnp.where(last_row, row, next_row[k]) - x
        diff_e = jnp.where(last_cell, cell, next_cell[k]) - x
        scale = lax.rsqrt(diff_a * diff_a + diff_b * diff_b + diff_e * diff_e + SMOOTHING)
        unit_a[k], unit_b[k], unit_e[k] = diff_a * scale, diff_b * scale, diff_e * scale
        slope[k] = unit_before[k] - (diff_a + diff_b + diff_e) * scale
    past_row = {k: pltpu.roll(x, 1, 0) for k, x in unit_b.items()}
    past_cell = {k: pltpu.roll(x, 1, 1) for k, x in unit_e.items()}
    for i, t in here:
        k = (i, t)
        rim = unit_at_rim(here[k]) if i == 0 or t == 0 else None
        row = past_row[i - 1, t] if i else rim
        cell = past_cell[i, t - 1] if t else rim
        slope[k] += jnp.where(first_row, row, past_row[k])
        slope[k] += jnp.where(first_cell, cell, past_cell[k])
    return slope, unit_a


def smooth_kernel(sizes, near_ref, far_ref, exact_ref, out_ref, seen_ref, field, slopes, units):
    slabs, bands, planes, rows, tiles, tvox = sizes
    slab, band = lax.axis_index("slab"), lax.axis_index("xy")
    depth, per = slabs * planes, rows // 8
    size = bands * per, tiles
    blocks = [(i, t) for i in range(size[0]) for t in range(size[1])]

    views, own, unit, tdet = exact_ref.shape
    for v in range(views):
        for i in range(own):
            for c in range(unit):
                at = (i * unit + c) * tdet
                seen_ref[v : v + 1, at : at + tdet] = exact_ref[v, i, c : c + 1, :]

    gap = jnp.zeros((rows, tvox), jnp.float32)
    for half, ref in enumerate((near_ref, far_ref)):
        for i, flip in enumerate(range(0, slabs, 2)):
            for j in range(bands):
                plane, at = (slab ^ (flip + half)) * planes, (band ^ j) * per
                for p in range(planes):
                    for t in range(tiles):
                        tile = ref[i, (j * planes + p) * tiles + t]
                        for n in range(per):
                            field[plane + p, at + n, t] = tile[8 * n : 8 * n + 8]
            gap += ref[i, bands * planes * tiles]
    nothing = jnp.zeros((8, tvox), jnp.float32)
    for i, t in blocks:
        field[depth, i, t] = nothing
        slopes[depth, i, t] = nothing
    row_ids = lax.broadcasted_iota(jnp.int32, (8, tvox), 0)
    cell_ids = lax.broadcasted_iota(jnp.int32, (8, tvox), 1)
    masks = (row_ids == 0, row_ids == 7, cell_ids == 0, cell_ids == tvox - 1)

    def total(square):
        return jnp.sum(jnp.sum(square, axis=0, keepdims=True), axis=1, keepdims=True)

    def finish(p, here, after, square):
        before = {(i, t): units[i, t] for i, t in blocks}
        slope, unit_a = slope_of(here, after, before, size, masks)
        for i, t in blocks:
            slopes[p, i, t] = slope[i, t]
            units[i, t] = unit_a[i, t]
            square = square + slope[i, t] * slope[i, t]
        return square

    norm = jnp.sqrt(total(gap))
    unroll = 4 if depth % 4 == 0 and len(blocks) <= 16 else 1

    def one(p, square):
        here = {(i, t): field[p, i, t] for i, t in blocks}
        after = {(i, t): field[p + 1, i, t] for i, t in blocks}
        return finish(p, here, after, square)

    for i, t in blocks:
        units[i, t] = unit_at_rim(field[0, i, t])
    square = lax.fori_loop(0, depth, one, nothing, unroll=unroll)
    step = TV_RATE * norm / jnp.sqrt(total(square) + 1e-06)

    def two(p, square):
        here = {(i, t): field[p, i, t] for i, t in blocks}
        after = {(i, t): field[p + 1, i, t] - step * slopes[p + 1, i, t] for i, t in blocks}
        for i, t in blocks:
            field[p + 1, i, t] = after[i, t]
        return finish(p, here, after, square)

    for i, t in blocks:
        here = field[0, i, t] - step * slopes[0, i, t]
        field[0, i, t] = here
        units[i, t] = unit_at_rim(here)
    square = lax.fori_loop(0, depth, two, nothing, unroll=unroll)
    step = TV_RATE * norm / jnp.sqrt(total(square) + 1e-06)
    for p in range(planes):
        for n in range(per):
            for t in range(tiles):
                at = slab * planes + p, band * per + n, t
                out_ref[p, 8 * n : 8 * n + 8, t * tvox : (t + 1) * tvox] = (
                    field[at] - step * slopes[at]
                )


def smooth(volume, near, far, exact, slabs, bands, tiles):
    planes, rows, cells = volume.shape
    views, own, unit, tdet = exact.shape
    sizes = slabs, bands, planes, rows, tiles, cells // tiles
    plane = bands * rows // 8, tiles, 8, cells // tiles
    return pl.pallas_call(
        functools.partial(smooth_kernel, sizes),
        out_shape=(
            jax.ShapeDtypeStruct(volume.shape, jnp.float32),
            jax.ShapeDtypeStruct((views, own * unit * tdet), jnp.float32),
        ),
        in_specs=in_vmem(3),
        out_specs=tuple(in_vmem(2)),
        scratch_shapes=[
            pltpu.VMEM((slabs * planes + 1,) + plane, jnp.float32),
            pltpu.VMEM((slabs * planes + 1,) + plane, jnp.float32),
            pltpu.VMEM(plane, jnp.float32),
        ],
        compiler_params=pltpu.CompilerParams(vmem_limit_bytes=VMEM_BYTES),
        name="smooth",
    )(near, far, exact)


def body(volume, footprint, tile_block, tile_cells, measured):
    views, tdet = footprint.shape[3], footprint.shape[5]
    slabs, bands = lax.axis_size("slab"), lax.axis_size("xy")
    plan = Plan(slabs, bands, views, measured.shape[1] // tdet, tdet)
    block, cells = (jnp.transpose(each, (0, 2, 3, 1)) for each in (tile_block, tile_cells))

    packed, low, high, seen, footprint = project(
        plan, volume, footprint, block, cells, measured
    )
    below, above = shift_all(high, "slab", 1), shift_all(low, "slab", -1)
    chunks = shares(plan, packed, below, above)
    parts = [
        swap_all(chunks[flip], "xy", flip) if flip else chunks[0] for flip in reduce_order(bands)
    ]
    exact, rounded = correct(plan, seen, parts)
    parts = [rounded] + [swap_all(rounded, "xy", flip) for flip in range(1, bands)]
    tiled = back_project(plan, volume, footprint, block, cells, parts)

    line = [tiled] + [swap_all(tiled, "xy", flip) for flip in range(1, bands)]
    line = jnp.concatenate([each[:-1] for each in line] + [sum(each[-1:] for each in line)])
    near = jnp.stack([line] + [swap_all(line, "slab", flip) for flip in range(2, slabs, 2)])
    far = swap_all(near, "slab", 1)
    return smooth(volume, near, far, exact, slabs, bands, footprint.shape[2])


def solution(mesh):
    placed = (
        P("slab", "xy", None),
        P("slab", "xy", None, None, None, None),
        P("slab", "xy", None, None),
        P("slab", "xy", None, None),
        P(),
    )
    return jax.shard_map(
        body,
        mesh=mesh,
        in_specs=placed,
        out_specs=(P("slab", "xy", None), P(None, ("slab", "xy"))),
        check_vma=False,
    )
```

```python
import functools

import jax
import jax.numpy as jnp
from jax import lax
from jax.experimental import pallas as pl
from jax.experimental.pallas import tpu as pltpu
from jax.sharding import PartitionSpec as P

RELAX = 1.0
TV_RATE = 0.8
SMOOTHING = 0.01
DCOLS = 2048
VMEM_BYTES = 32 * 1024 * 1024


class Plan:
    def __init__(self, slabs, bands, views, nblocks, tdet):
        self.slabs, self.bands, self.views, self.tdet = slabs, bands, views, tdet
        per_row = DCOLS // tdet
        own = nblocks // (slabs * bands)
        self.slab_own = nblocks // slabs
        self.halo = per_row
        self.unit = min(per_row, own)
        self.own_units = own // self.unit
        self.halo_units = per_row // self.unit
        self.units = self.slab_own // self.unit + 2 * self.halo_units
        self.chunk = self.own_units + self.halo_units
        narrow = per_row // bands
        fits = self.unit == per_row and narrow * bands == per_row and narrow + 2 < per_row
        self.narrow = narrow if fits else 0
        self.width = [
            self.narrow + 2 if v % 2 and self.narrow else self.unit for v in range(views)
        ]
        self.base = [2 * sum(self.width[:v]) for v in range(views)]
        self.lines = 2 * sum(self.width)

    def is_narrow(self, v):
        return self.width[v] != self.unit


def shift_all(cells, axis, step):
    count = lax.axis_size(axis)
    return lax.ppermute(cells, axis, [(i, (i + step) % count) for i in range(count)])


def reduce_order(bands):
    return [0] + [flip for flip in (3, 1, 2) if flip < bands] + list(range(4, bands))


def swap_all(cells, axis, flip):
    count = lax.axis_size(axis)
    return lax.ppermute(cells, axis, [(i, i ^ flip) for i in range(count)])


def unit_of(plan, block, slab):
    local = jnp.clip(
        block - slab * plan.slab_own + plan.halo, 0, plan.units * plan.unit - 1
    )
    return lax.div(local, plan.unit), lax.rem(local, plan.unit)


def copy_all(pairs, sems):
    return [pltpu.make_async_copy(src, dst, sems.at[n]) for n, (src, dst) in enumerate(pairs)]


def stream_spans(planes, rows):
    size = max(rows // 4, 1)
    return [(p, r, min(size, rows - r)) for p in range(planes) for r in range(0, rows, size)]


def project_kernel(
    plan, shape, vol_hbm, foot_hbm, block_hbm, cells_hbm, seen_hbm,
    out_ref, low_ref, high_ref, seen_ref, foot, acc, vol_ref, block_ref, cells_ref, seen, sems, small,
):
    planes, rows, tiles, views, tvox, tdet = shape
    slab, band = lax.axis_index("slab"), lax.axis_index("xy")
    spans = stream_spans(planes, rows)
    span = plan.unit * tdet
    own_at = (slab * plan.bands + band) * plan.own_units
    halo_at = jnp.where(
        band == 0,
        slab * (plan.slab_own // plan.unit) - plan.halo_units,
        (slab + 1) * (plan.slab_own // plan.unit),
    )
    halo_at = jnp.clip(halo_at, 0, seen_hbm.shape[1] // span - plan.halo_units)
    own_at, halo_at = (pl.multiple_of(at * span, span) for at in (own_at, halo_at))
    own_size, halo_size = plan.own_units * span, plan.halo_units * span
    first = copy_all(
        [
            (block_hbm, block_ref),
            (cells_hbm, cells_ref),
            (vol_hbm, vol_ref),
            (seen_hbm.at[:, pl.ds(own_at, own_size)], seen.at[:, pl.ds(0, own_size)]),
            (seen_hbm.at[:, pl.ds(halo_at, halo_size)], seen.at[:, pl.ds(own_size, halo_size)]),
        ],
        small,
    )
    stream = [(foot_hbm.at[p, pl.ds(r, n)], foot.at[p, pl.ds(r, n)]) for p, r, n in spans]
    stream = copy_all(stream, sems)
    for copy in first:
        copy.start()
    for copy in stream:
        copy.start(priority=1)
    acc[...] = jnp.zeros_like(acc)
    top = lax.broadcasted_iota(jnp.int32, (8, tvox), 0) == 0
    lane = lax.broadcasted_iota(jnp.int32, (8, tdet), 1)
    for copy in first:
        copy.wait()
    for v in range(views):
        for i in range(plan.chunk):
            for c in range(plan.unit):
                at = (i * plan.unit + c) * tdet
                seen_ref[v, i, c : c + 1, :] = seen[v : v + 1, at : at + tdet]
    starts = [plan.units * sum(plan.width[:v]) for v in range(views)]
    for copy, (p, begin, size) in zip(stream, spans):
        copy.wait()
        for r in range(begin, begin + size):
            for t in range(tiles):
                voxels = vol_ref[p, r : r + 1, t * tvox : (t + 1) * tvox]
                left = jnp.where(top, jnp.broadcast_to(voxels, (8, tvox)), 1.0)
                left = left.astype(jnp.bfloat16)
                for v in range(views):
                    sums = jnp.dot(left, foot[p, r, t, v], preferred_element_type=jnp.float32)
                    sums = jnp.where(lane < cells_ref[p, t, v, r], sums, 0.0)
                    unit, column = unit_of(plan, block_ref[p, t, v, r], slab)
                    if plan.is_narrow(v):
                        column = column - (band * plan.narrow - 1)
                        column = jnp.clip(column, 0, plan.width[v] - 1)
                    acc[starts[v] + unit * plan.width[v] + column] += sums
    for unit in range(plan.units):
        for v in range(views):
            width = plan.width[v]
            at = starts[v] + unit * width
            for q in range(2):
                line = plan.base[v] + q * width
                out_ref[unit, line : line + width, :] = acc[at : at + width, q, :]
    edge = 2 * plan.halo_units
    low_ref[...] = out_ref[:edge]
    high_ref[...] = out_ref[plan.units - edge :]


def in_vmem(count):
    return [pl.BlockSpec(memory_space=pltpu.VMEM)] * count


def project(plan, volume, footprint, tile_block, tile_cells, measured):
    shape = footprint.shape
    views, tdet = plan.views, plan.tdet
    parts = len(stream_spans(*shape[:2]))
    operands = [
        pltpu.with_memory_space_constraint(operand, pltpu.HBM)
        for operand in (volume, footprint, tile_block, tile_cells, measured)
    ]
    border = (2 * plan.halo_units, plan.lines, tdet)
    return pl.pallas_call(
        functools.partial(project_kernel, plan, shape),
        out_shape=(
            jax.ShapeDtypeStruct((plan.units, plan.lines, tdet), jnp.float32),
            jax.ShapeDtypeStruct(border, jnp.float32),
            jax.ShapeDtypeStruct(border, jnp.float32),
            jax.ShapeDtypeStruct((views, plan.chunk, plan.unit, tdet), jnp.float32),
            pltpu.VMEM(shape, jnp.bfloat16),
        ),
        in_specs=[pl.BlockSpec(memory_space=pltpu.HBM)] * 5,
        out_specs=tuple(in_vmem(5)),
        scratch_shapes=[
            pltpu.VMEM((plan.units * sum(plan.width), 8, tdet), jnp.float32),
            pltpu.VMEM(volume.shape, jnp.float32),
            pltpu.SMEM(tile_block.shape, jnp.int32),
            pltpu.SMEM(tile_cells.shape, jnp.int32),
            pltpu.VMEM((views, plan.chunk * plan.unit * tdet), jnp.float32),
            pltpu.SemaphoreType.DMA((parts,)),
            pltpu.SemaphoreType.DMA((5,)),
        ],
        compiler_params=pltpu.CompilerParams(vmem_limit_bytes=VMEM_BYTES),
        name="project",
    )(*operands)


def share_kernel(plan, packed_ref, below_ref, above_ref, *rest):
    out_refs, total = rest[:-1], rest[-1]
    slab, band = lax.axis_index("slab"), lax.axis_index("xy")
    edge = 2 * plan.halo_units
    total[...] = packed_ref[...]
    total[:edge] += jnp.where(slab == 0, 0.0, below_ref[...])
    total[plan.units - edge :] += jnp.where(slab == plan.slabs - 1, 0.0, above_ref[...])
    for flip, out_ref in enumerate(out_refs):
        owner = band ^ flip
        for i in range(plan.own_units):
            out_ref[i] = total[plan.halo_units + owner * plan.own_units + i]
        halo = jnp.where(owner == 0, 0, plan.units - plan.halo_units)
        for i in range(plan.halo_units):
            out_ref[plan.own_units + i] = total[halo + i]


def shares(plan, packed, below, above):
    chunk = jax.ShapeDtypeStruct((plan.chunk,) + packed.shape[1:], jnp.float32)
    return pl.pallas_call(
        functools.partial(share_kernel, plan),
        out_shape=(chunk,) * plan.bands,
        in_specs=in_vmem(3),
        out_specs=tuple(in_vmem(plan.bands)),
        scratch_shapes=[pltpu.VMEM(packed.shape, jnp.float32)],
        compiler_params=pltpu.CompilerParams(vmem_limit_bytes=VMEM_BYTES // 4),
        name="shares",
    )(packed, below, above)


def correct_kernel(plan, seen_ref, ready_ref, *rest):
    del ready_ref
    parts, (exact_ref, rounded_ref) = rest[:-2], rest[-2:]
    band = lax.axis_index("xy")
    tdet, unit = plan.tdet, plan.unit
    rounded = []
    for v in range(plan.views):
        width = plan.width[v]
        for i in range(plan.chunk):
            sums = []
            for q in range(2):
                line = plan.base[v] + q * width
                total = 0.0
                for flip, part in zip(reduce_order(plan.bands), parts):
                    piece = part[i, line : line + width, :]
                    if plan.is_narrow(v):
                        room = jnp.zeros((unit - width, tdet), jnp.float32)
                        piece = jnp.concatenate([piece, room], axis=0)
                        first = (band ^ flip) * plan.narrow - 1
                        piece = pltpu.roll(piece, lax.rem(first + unit, unit), 0)
                    total = total + piece
                sums.append(total)
            corrected = (seen_ref[v, i] - sums[0]) / jnp.maximum(sums[1], 1.0)
            rounded.append(corrected)
            if i < plan.own_units:
                exact_ref[v, i] = corrected
    rounded_ref[...] = jnp.concatenate(rounded, axis=0).astype(jnp.bfloat16)


def correct(plan, seen, parts, ready):
    views, chunk, unit, tdet = seen.shape
    return pl.pallas_call(
        functools.partial(correct_kernel, plan),
        out_shape=(
            jax.ShapeDtypeStruct((views, plan.own_units, unit, tdet), jnp.float32),
            jax.ShapeDtypeStruct((views * chunk * unit, tdet), jnp.bfloat16),
        ),
        in_specs=in_vmem(1) + [pl.BlockSpec(memory_space=pl.ANY)] + in_vmem(len(parts)),
        out_specs=tuple(in_vmem(2)),
        compiler_params=pltpu.CompilerParams(vmem_limit_bytes=VMEM_BYTES // 4),
        name="correct",
    )(seen, ready, *parts)


def turn_kernel(shape, foot, turned):
    for p in range(shape[0]):
        for r in range(shape[1]):
            for t in range(shape[2]):
                for v in range(shape[3]):
                    turned[p, r, t, v] = foot[p, r, t, v].T


def turn(footprint):
    shape = footprint.shape
    footprint = pltpu.with_memory_space_constraint(footprint, pltpu.VMEM)
    return pl.pallas_call(
        functools.partial(turn_kernel, shape),
        out_shape=pltpu.VMEM(shape[:4] + (shape[5], shape[4]), jnp.bfloat16),
        in_specs=in_vmem(1),
        out_specs=pl.BlockSpec(memory_space=pltpu.VMEM),
        compiler_params=pltpu.CompilerParams(vmem_limit_bytes=VMEM_BYTES // 4),
        cost_estimate=pl.CostEstimate(
            flops=0, bytes_accessed=4 * footprint.size, transcendentals=0
        ),
        name="turn",
    )(footprint)


def back_kernel(plan, shape, vol_any, foot, block_any, cells_any, *rest):
    parts, (out_ref, sums, corr, vol_ref, block_ref, cells_ref, small) = rest[:-7], rest[-7:]
    planes, rows, tiles, views, tvox, tdet = shape
    slab, band = lax.axis_index("slab"), lax.axis_index("xy")
    first = copy_all([(block_any, block_ref), (cells_any, cells_ref), (vol_any, vol_ref)], small)
    for copy in first:
        copy.start()
    for flip, part in zip([0] + list(range(plan.bands - 1, 0, -1)), parts):
        source = band ^ flip
        piece = part[...].astype(jnp.float32).reshape(views, plan.chunk, plan.unit, tdet)
        halo = jnp.where(
            source == 0,
            0,
            jnp.where(source == plan.bands - 1, plan.units - plan.halo_units, plan.units),
        )
        for v in range(views):
            for i in range(plan.own_units):
                corr[v, plan.halo_units + source * plan.own_units + i] = piece[v, i]
            for i in range(plan.halo_units):
                corr[v, halo + i] = piece[v, plan.own_units + i]
    top = lax.broadcasted_iota(jnp.int32, (8, tdet), 0) == 0
    lane = lax.broadcasted_iota(jnp.int32, (8, tdet), 1)
    for copy in first:
        copy.wait()
    gap_sum = jnp.zeros((rows, tvox), jnp.float32)
    for p in range(planes):
        for t in range(tiles):
            for r in range(rows):
                both = 0.0
                for v in range(views):
                    unit, column = unit_of(plan, block_ref[p, t, v, r], slab)
                    picked = jnp.broadcast_to(corr[v, unit, pl.ds(column, 1), :], (8, tdet))
                    left = jnp.where(top, picked, 1.0)
                    left = jnp.where(lane < cells_ref[p, t, v, r], left, 0.0).astype(jnp.bfloat16)
                    both += jnp.dot(left, foot[p, r, t, v], preferred_element_type=jnp.float32)
                sums[0, r : r + 1] = both[0:1]
                sums[1, r : r + 1] = both[1:2]
            volume = vol_ref[p, :, t * tvox : (t + 1) * tvox]
            sart = jnp.maximum(volume + RELAX * (sums[0] / sums[1]), 0.0)
            out_ref[p * tiles + t] = sart
            gap = sart - volume
            gap_sum += gap * gap
    out_ref[planes * tiles] = gap_sum


def back_project(plan, volume, footprint, tile_block, tile_cells, parts):
    planes, rows, tiles, views, tdet, tvox = footprint.shape
    shape = planes, rows, tiles, views, tvox, tdet
    spaces = [pl.ANY, pltpu.VMEM, pl.ANY, pl.ANY] + [pltpu.VMEM] * len(parts)
    footprint = pltpu.with_memory_space_constraint(footprint, pltpu.VMEM)
    return pl.pallas_call(
        functools.partial(back_kernel, plan, shape),
        out_shape=jax.ShapeDtypeStruct((planes * tiles + 1, rows, tvox), jnp.float32),
        in_specs=[pl.BlockSpec(memory_space=space) for space in spaces],
        out_specs=pl.BlockSpec(memory_space=pltpu.VMEM),
        scratch_shapes=[
            pltpu.VMEM((2, rows, tvox), jnp.float32),
            pltpu.VMEM((views, plan.units + plan.halo_units, plan.unit, tdet), jnp.float32),
            pltpu.VMEM(volume.shape, jnp.float32),
            pltpu.SMEM(tile_block.shape, jnp.int32),
            pltpu.SMEM(tile_cells.shape, jnp.int32),
            pltpu.SemaphoreType.DMA((3,)),
        ],
        compiler_params=pltpu.CompilerParams(vmem_limit_bytes=VMEM_BYTES // 2),
        name="back_project",
    )(volume, footprint, tile_block, tile_cells, *parts)


def unit_at_rim(cells):
    return cells * lax.rsqrt(cells * cells + SMOOTHING)


def slope_of(here, after, unit_before, size, masks):
    high, wide = size
    first_row, last_row, first_cell, last_cell = masks
    lanes = here[0, 0].shape[1]
    next_row = {k: pltpu.roll(x, 7, 0) for k, x in here.items()}
    next_cell = {k: pltpu.roll(x, lanes - 1, 1) for k, x in here.items()}
    slope, unit_a, unit_b, unit_e = {}, {}, {}, {}
    for i, t in here:
        k, x = (i, t), here[i, t]
        row = next_row[i + 1, t] if i + 1 < high else 0.0
        cell = next_cell[i, t + 1] if t + 1 < wide else 0.0
        diff_a = after[k] - x
        diff_b = jnp.where(last_row, row, next_row[k]) - x
        diff_e = jnp.where(last_cell, cell, next_cell[k]) - x
        scale = lax.rsqrt(diff_a * diff_a + diff_b * diff_b + diff_e * diff_e + SMOOTHING)
        unit_a[k], unit_b[k], unit_e[k] = diff_a * scale, diff_b * scale, diff_e * scale
        slope[k] = unit_before[k] - (diff_a + diff_b + diff_e) * scale
    past_row = {k: pltpu.roll(x, 1, 0) for k, x in unit_b.items()}
    past_cell = {k: pltpu.roll(x, 1, 1) for k, x in unit_e.items()}
    for i, t in here:
        k = (i, t)
        rim = unit_at_rim(here[k]) if i == 0 or t == 0 else None
        row = past_row[i - 1, t] if i else rim
        cell = past_cell[i, t - 1] if t else rim
        slope[k] += jnp.where(first_row, row, past_row[k])
        slope[k] += jnp.where(first_cell, cell, past_cell[k])
    return slope, unit_a


def smooth_kernel(sizes, near_ref, far_ref, exact_ref, out_ref, seen_ref, field, slopes, units):
    slabs, bands, planes, rows, tiles, tvox = sizes
    slab, band = lax.axis_index("slab"), lax.axis_index("xy")
    depth, per = slabs * planes, rows // 8
    size = bands * per, tiles
    blocks = [(i, t) for i in range(size[0]) for t in range(size[1])]

    views, own, unit, tdet = exact_ref.shape
    for v in range(views):
        for i in range(own):
            for c in range(unit):
                at = (i * unit + c) * tdet
                seen_ref[v : v + 1, at : at + tdet] = exact_ref[v, i, c : c + 1, :]

    gap = jnp.zeros((rows, tvox), jnp.float32)
    for half, ref in enumerate((near_ref, far_ref)):
        for i, flip in enumerate([0] + list(range(slabs - 2, 0, -2))):
            for j in range(bands):
                plane, at = (slab ^ (flip + half)) * planes, (band ^ ((bands - j) % bands)) * per
                for p in range(planes):
                    for t in range(tiles):
                        tile = ref[i, (j * planes + p) * tiles + t]
                        for n in range(per):
                            field[plane + p, at + n, t] = tile[8 * n : 8 * n + 8]
            gap += ref[i, bands * planes * tiles]
    nothing = jnp.zeros((8, tvox), jnp.float32)
    for i, t in blocks:
        field[depth, i, t] = nothing
        slopes[depth, i, t] = nothing
    row_ids = lax.broadcasted_iota(jnp.int32, (8, tvox), 0)
    cell_ids = lax.broadcasted_iota(jnp.int32, (8, tvox), 1)
    masks = (row_ids == 0, row_ids == 7, cell_ids == 0, cell_ids == tvox - 1)

    def total(square):
        return jnp.sum(jnp.sum(square, axis=0, keepdims=True), axis=1, keepdims=True)

    def finish(p, here, after, square):
        before = {(i, t): units[i, t] for i, t in blocks}
        slope, unit_a = slope_of(here, after, before, size, masks)
        for i, t in blocks:
            slopes[p, i, t] = slope[i, t]
            units[i, t] = unit_a[i, t]
            square = square + slope[i, t] * slope[i, t]
        return square

    norm = jnp.sqrt(total(gap))
    unroll = 4 if depth % 4 == 0 and len(blocks) <= 16 else 1

    def one(p, square):
        here = {(i, t): field[p, i, t] for i, t in blocks}
        after = {(i, t): field[p + 1, i, t] for i, t in blocks}
        return finish(p, here, after, square)

    for i, t in blocks:
        units[i, t] = unit_at_rim(field[0, i, t])
    square = lax.fori_loop(0, depth, one, nothing, unroll=unroll)
    step = TV_RATE * norm / jnp.sqrt(total(square) + 1e-06)

    def two(p, square):
        here = {(i, t): field[p, i, t] for i, t in blocks}
        after = {(i, t): field[p + 1, i, t] - step * slopes[p + 1, i, t] for i, t in blocks}
        for i, t in blocks:
            field[p + 1, i, t] = after[i, t]
        return finish(p, here, after, square)

    for i, t in blocks:
        here = field[0, i, t] - step * slopes[0, i, t]
        field[0, i, t] = here
        units[i, t] = unit_at_rim(here)
    square = lax.fori_loop(0, depth, two, nothing, unroll=unroll)
    step = TV_RATE * norm / jnp.sqrt(total(square) + 1e-06)
    for p in range(planes):
        for n in range(per):
            for t in range(tiles):
                at = slab * planes + p, band * per + n, t
                out_ref[p, 8 * n : 8 * n + 8, t * tvox : (t + 1) * tvox] = (
                    field[at] - step * slopes[at]
                )


def smooth(volume, near, far, exact, slabs, bands, tiles):
    planes, rows, cells = volume.shape
    views, own, unit, tdet = exact.shape
    sizes = slabs, bands, planes, rows, tiles, cells // tiles
    plane = bands * rows // 8, tiles, 8, cells // tiles
    return pl.pallas_call(
        functools.partial(smooth_kernel, sizes),
        out_shape=(
            jax.ShapeDtypeStruct(volume.shape, jnp.float32),
            jax.ShapeDtypeStruct((views, own * unit * tdet), jnp.float32),
        ),
        in_specs=in_vmem(3),
        out_specs=tuple(in_vmem(2)),
        scratch_shapes=[
            pltpu.VMEM((slabs * planes + 1,) + plane, jnp.float32),
            pltpu.VMEM((slabs * planes + 1,) + plane, jnp.float32),
            pltpu.VMEM(plane, jnp.float32),
        ],
        compiler_params=pltpu.CompilerParams(vmem_limit_bytes=VMEM_BYTES),
        name="smooth",
    )(near, far, exact)


def body(volume, footprint, tile_block, tile_cells, measured):
    views, tdet = footprint.shape[3], footprint.shape[5]
    slabs, bands = lax.axis_size("slab"), lax.axis_size("xy")
    plan = Plan(slabs, bands, views, measured.shape[1] // tdet, tdet)
    block, cells = (jnp.transpose(each, (0, 2, 3, 1)) for each in (tile_block, tile_cells))

    packed, low, high, seen, footprint = project(
        plan, volume, footprint, block, cells, measured
    )
    below, above = shift_all(high, "slab", 1), shift_all(low, "slab", -1)
    chunks = shares(plan, packed, below, above)
    parts = [
        swap_all(chunks[flip], "xy", flip) if flip else chunks[0] for flip in reduce_order(bands)
    ]
    turned = turn(footprint)
    exact, rounded = correct(plan, seen, parts, turned)
    parts = [rounded] + [swap_all(rounded, "xy", flip) for flip in range(bands - 1, 0, -1)]
    tiled = back_project(plan, volume, turned, block, cells, parts)

    line = [tiled] + [swap_all(tiled, "xy", flip) for flip in range(bands - 1, 0, -1)]
    line = jnp.concatenate([each[:-1] for each in line] + [sum(each[-1:] for each in line)])
    near = jnp.stack([line] + [swap_all(line, "slab", flip) for flip in range(slabs - 2, 0, -2)])
    far = swap_all(near, "slab", 1)
    return smooth(volume, near, far, exact, slabs, bands, footprint.shape[2])


def solution(mesh):
    placed = (
        P("slab", "xy", None),
        P("slab", "xy", None, None, None, None),
        P("slab", "xy", None, None),
        P("slab", "xy", None, None),
        P(),
    )
    return jax.shard_map(
        body,
        mesh=mesh,
        in_specs=placed,
        out_specs=(P("slab", "xy", None), P(None, ("slab", "xy"))),
        check_vma=False,
    )
```

```python
import functools

import jax
import jax.numpy as jnp
from jax import lax
from jax.experimental import pallas as pl
from jax.experimental.pallas import tpu as pltpu
from jax.sharding import PartitionSpec as P

RELAX = 1.0
TV_RATE = 0.8
SMOOTHING = 0.01
DCOLS = 2048
VMEM_BYTES = 32 * 1024 * 1024


class Plan:
    def __init__(self, slabs, bands, views, nblocks, tdet):
        self.slabs, self.bands, self.views, self.tdet = slabs, bands, views, tdet
        per_row = DCOLS // tdet
        own = nblocks // (slabs * bands)
        self.slab_own = nblocks // slabs
        self.halo = per_row
        self.unit = min(per_row, own)
        self.own_units = own // self.unit
        self.halo_units = per_row // self.unit
        self.units = self.slab_own // self.unit + 2 * self.halo_units
        self.chunk = self.own_units + self.halo_units
        narrow = per_row // bands
        fits = self.unit == per_row and narrow * bands == per_row and narrow + 2 < per_row
        self.narrow = narrow if fits else 0
        self.width = [
            self.narrow + 2 if v % 2 and self.narrow else self.unit for v in range(views)
        ]
        self.base = [2 * sum(self.width[:v]) for v in range(views)]
        self.lines = 2 * sum(self.width)

    def is_narrow(self, v):
        return self.width[v] != self.unit


def shift_all(cells, axis, step):
    count = lax.axis_size(axis)
    return lax.ppermute(cells, axis, [(i, (i + step) % count) for i in range(count)])


def reduce_order(bands):
    return [0] + [flip for flip in (3, 1, 2) if flip < bands] + list(range(4, bands))


def swap_all(cells, axis, flip):
    count = lax.axis_size(axis)
    return lax.ppermute(cells, axis, [(i, i ^ flip) for i in range(count)])


def unit_of(plan, block, slab):
    local = jnp.clip(
        block - slab * plan.slab_own + plan.halo, 0, plan.units * plan.unit - 1
    )
    return lax.div(local, plan.unit), lax.rem(local, plan.unit)


def copy_all(pairs, sems):
    return [pltpu.make_async_copy(src, dst, sems.at[n]) for n, (src, dst) in enumerate(pairs)]


def stream_spans(planes, rows):
    size = max(rows // 4, 1)
    return [(p, r, min(size, rows - r)) for p in range(planes) for r in range(0, rows, size)]


def project_kernel(
    plan, shape, vol_hbm, foot_hbm, block_hbm, cells_hbm, seen_hbm,
    out_ref, low_ref, high_ref, seen_ref, foot, acc, vol_ref, block_ref, cells_ref, seen, sems, small,
):
    planes, rows, tiles, views, tvox, tdet = shape
    slab, band = lax.axis_index("slab"), lax.axis_index("xy")
    spans = stream_spans(planes, rows)
    span = plan.unit * tdet
    own_at = (slab * plan.bands + band) * plan.own_units
    halo_at = jnp.where(
        band == 0,
        slab * (plan.slab_own // plan.unit) - plan.halo_units,
        (slab + 1) * (plan.slab_own // plan.unit),
    )
    halo_at = jnp.clip(halo_at, 0, seen_hbm.shape[1] // span - plan.halo_units)
    own_at, halo_at = (pl.multiple_of(at * span, span) for at in (own_at, halo_at))
    own_size, halo_size = plan.own_units * span, plan.halo_units * span
    first = copy_all(
        [
            (block_hbm, block_ref),
            (cells_hbm, cells_ref),
            (vol_hbm, vol_ref),
            (seen_hbm.at[:, pl.ds(own_at, own_size)], seen.at[:, pl.ds(0, own_size)]),
            (seen_hbm.at[:, pl.ds(halo_at, halo_size)], seen.at[:, pl.ds(own_size, halo_size)]),
        ],
        small,
    )
    stream = [(foot_hbm.at[p, pl.ds(r, n)], foot.at[p, pl.ds(r, n)]) for p, r, n in spans]
    stream = copy_all(stream, sems)
    for copy in first:
        copy.start()
    for copy in stream:
        copy.start(priority=1)
    acc[...] = jnp.zeros_like(acc)
    top = lax.broadcasted_iota(jnp.int32, (8, tvox), 0) == 0
    lane = lax.broadcasted_iota(jnp.int32, (8, tdet), 1)
    for copy in first:
        copy.wait()
    for v in range(views):
        for i in range(plan.chunk):
            for c in range(plan.unit):
                at = (i * plan.unit + c) * tdet
                seen_ref[v, i, c : c + 1, :] = seen[v : v + 1, at : at + tdet]
    starts = [plan.units * sum(plan.width[:v]) for v in range(views)]
    for copy, (p, begin, size) in zip(stream, spans):
        copy.wait()
        for r in range(begin, begin + size):
            for t in range(tiles):
                voxels = vol_ref[p, r : r + 1, t * tvox : (t + 1) * tvox]
                left = jnp.where(top, jnp.broadcast_to(voxels, (8, tvox)), 1.0)
                left = left.astype(jnp.bfloat16)
                for v in range(views):
                    sums = jnp.dot(left, foot[p, r, t, v], preferred_element_type=jnp.float32)
                    sums = jnp.where(lane < cells_ref[p, t, v, r], sums, 0.0)
                    unit, column = unit_of(plan, block_ref[p, t, v, r], slab)
                    if plan.is_narrow(v):
                        column = column - (band * plan.narrow - 1)
                        column = jnp.clip(column, 0, plan.width[v] - 1)
                    acc[starts[v] + unit * plan.width[v] + column] += sums
    for unit in range(plan.units):
        for v in range(views):
            width = plan.width[v]
            at = starts[v] + unit * width
            for q in range(2):
                line = plan.base[v] + q * width
                out_ref[unit, line : line + width, :] = acc[at : at + width, q, :]
    edge = 2 * plan.halo_units
    low_ref[...] = out_ref[:edge]
    high_ref[...] = out_ref[plan.units - edge :]


def in_vmem(count):
    return [pl.BlockSpec(memory_space=pltpu.VMEM)] * count


def project(plan, volume, footprint, tile_block, tile_cells, measured):
    shape = footprint.shape
    views, tdet = plan.views, plan.tdet
    parts = len(stream_spans(*shape[:2]))
    operands = [
        pltpu.with_memory_space_constraint(operand, pltpu.HBM)
        for operand in (volume, footprint, tile_block, tile_cells, measured)
    ]
    border = (2 * plan.halo_units, plan.lines, tdet)
    return pl.pallas_call(
        functools.partial(project_kernel, plan, shape),
        out_shape=(
            jax.ShapeDtypeStruct((plan.units, plan.lines, tdet), jnp.float32),
            jax.ShapeDtypeStruct(border, jnp.float32),
            jax.ShapeDtypeStruct(border, jnp.float32),
            jax.ShapeDtypeStruct((views, plan.chunk, plan.unit, tdet), jnp.float32),
            pltpu.VMEM(shape, jnp.bfloat16),
        ),
        in_specs=[pl.BlockSpec(memory_space=pltpu.HBM)] * 5,
        out_specs=tuple(in_vmem(5)),
        scratch_shapes=[
            pltpu.VMEM((plan.units * sum(plan.width), 8, tdet), jnp.float32),
            pltpu.VMEM(volume.shape, jnp.float32),
            pltpu.SMEM(tile_block.shape, jnp.int32),
            pltpu.SMEM(tile_cells.shape, jnp.int32),
            pltpu.VMEM((views, plan.chunk * plan.unit * tdet), jnp.float32),
            pltpu.SemaphoreType.DMA((parts,)),
            pltpu.SemaphoreType.DMA((5,)),
        ],
        compiler_params=pltpu.CompilerParams(vmem_limit_bytes=VMEM_BYTES),
        name="project",
    )(*operands)


def share_kernel(plan, packed_ref, below_ref, above_ref, *rest):
    out_refs, total = rest[:-1], rest[-1]
    slab, band = lax.axis_index("slab"), lax.axis_index("xy")
    edge = 2 * plan.halo_units
    total[...] = packed_ref[...]
    total[:edge] += jnp.where(slab == 0, 0.0, below_ref[...])
    total[plan.units - edge :] += jnp.where(slab == plan.slabs - 1, 0.0, above_ref[...])
    for flip, out_ref in enumerate(out_refs):
        owner = band ^ flip
        for i in range(plan.own_units):
            out_ref[i] = total[plan.halo_units + owner * plan.own_units + i]
        halo = jnp.where(owner == 0, 0, plan.units - plan.halo_units)
        for i in range(plan.halo_units):
            out_ref[plan.own_units + i] = total[halo + i]


def shares(plan, packed, below, above):
    chunk = jax.ShapeDtypeStruct((plan.chunk,) + packed.shape[1:], jnp.float32)
    return pl.pallas_call(
        functools.partial(share_kernel, plan),
        out_shape=(chunk,) * plan.bands,
        in_specs=in_vmem(3),
        out_specs=tuple(in_vmem(plan.bands)),
        scratch_shapes=[pltpu.VMEM(packed.shape, jnp.float32)],
        compiler_params=pltpu.CompilerParams(vmem_limit_bytes=VMEM_BYTES // 4),
        name="shares",
    )(packed, below, above)


def correct_kernel(plan, seen_ref, ready_ref, *rest):
    del ready_ref
    parts, (exact_ref, rounded_ref) = rest[:-2], rest[-2:]
    band = lax.axis_index("xy")
    tdet, unit = plan.tdet, plan.unit
    rounded = []
    for v in range(plan.views):
        width = plan.width[v]
        for i in range(plan.chunk):
            sums = []
            for q in range(2):
                line = plan.base[v] + q * width
                total = 0.0
                for flip, part in zip(reduce_order(plan.bands), parts):
                    piece = part[i, line : line + width, :]
                    if plan.is_narrow(v):
                        room = jnp.zeros((unit - width, tdet), jnp.float32)
                        piece = jnp.concatenate([piece, room], axis=0)
                        first = (band ^ flip) * plan.narrow - 1
                        piece = pltpu.roll(piece, lax.rem(first + unit, unit), 0)
                    total = total + piece
                sums.append(total)
            corrected = (seen_ref[v, i] - sums[0]) / jnp.maximum(sums[1], 1.0)
            rounded.append(corrected)
            if i < plan.own_units:
                exact_ref[v, i] = corrected
    rounded_ref[...] = jnp.concatenate(rounded, axis=0).astype(jnp.bfloat16)


def correct(plan, seen, parts, ready):
    views, chunk, unit, tdet = seen.shape
    return pl.pallas_call(
        functools.partial(correct_kernel, plan),
        out_shape=(
            jax.ShapeDtypeStruct((views, plan.own_units, unit, tdet), jnp.float32),
            jax.ShapeDtypeStruct((views * chunk * unit, tdet), jnp.bfloat16),
        ),
        in_specs=in_vmem(1) + [pl.BlockSpec(memory_space=pl.ANY)] + in_vmem(len(parts)),
        out_specs=tuple(in_vmem(2)),
        compiler_params=pltpu.CompilerParams(vmem_limit_bytes=VMEM_BYTES // 4),
        name="correct",
    )(seen, ready, *parts)


def turn_kernel(shape, foot, turned):
    for p in range(shape[0]):
        for r in range(shape[1]):
            for t in range(shape[2]):
                for v in range(shape[3]):
                    turned[p, r, t, v] = foot[p, r, t, v].T


def turn(footprint):
    shape = footprint.shape
    footprint = pltpu.with_memory_space_constraint(footprint, pltpu.VMEM)
    return pl.pallas_call(
        functools.partial(turn_kernel, shape),
        out_shape=pltpu.VMEM(shape[:4] + (shape[5], shape[4]), jnp.bfloat16),
        in_specs=in_vmem(1),
        out_specs=pl.BlockSpec(memory_space=pltpu.VMEM),
        compiler_params=pltpu.CompilerParams(vmem_limit_bytes=VMEM_BYTES // 4),
        cost_estimate=pl.CostEstimate(
            flops=0, bytes_accessed=4 * footprint.size, transcendentals=0
        ),
        name="turn",
    )(footprint)


def back_kernel(plan, shape, vol_any, foot, block_any, cells_any, *rest):
    parts, (out_ref, sums, corr, vol_ref, block_ref, cells_ref, small) = rest[:-7], rest[-7:]
    planes, rows, tiles, views, tvox, tdet = shape
    slab, band = lax.axis_index("slab"), lax.axis_index("xy")
    first = copy_all([(block_any, block_ref), (cells_any, cells_ref), (vol_any, vol_ref)], small)
    for copy in first:
        copy.start()
    for flip, part in enumerate(parts):
        source = band ^ flip
        piece = part[...].astype(jnp.float32).reshape(views, plan.chunk, plan.unit, tdet)
        halo = jnp.where(
            source == 0,
            0,
            jnp.where(source == plan.bands - 1, plan.units - plan.halo_units, plan.units),
        )
        for v in range(views):
            for i in range(plan.own_units):
                corr[v, plan.halo_units + source * plan.own_units + i] = piece[v, i]
            for i in range(plan.halo_units):
                corr[v, halo + i] = piece[v, plan.own_units + i]
    top = lax.broadcasted_iota(jnp.int32, (8, tdet), 0) == 0
    lane = lax.broadcasted_iota(jnp.int32, (8, tdet), 1)
    for copy in first:
        copy.wait()
    gap_sum = jnp.zeros((rows, tvox), jnp.float32)
    for p in range(planes):
        for t in range(tiles):
            for r in range(rows):
                both = 0.0
                for v in range(views):
                    unit, column = unit_of(plan, block_ref[p, t, v, r], slab)
                    picked = jnp.broadcast_to(corr[v, unit, pl.ds(column, 1), :], (8, tdet))
                    left = jnp.where(top, picked, 1.0)
                    left = jnp.where(lane < cells_ref[p, t, v, r], left, 0.0).astype(jnp.bfloat16)
                    both += jnp.dot(left, foot[p, r, t, v], preferred_element_type=jnp.float32)
                sums[0, r : r + 1] = both[0:1]
                sums[1, r : r + 1] = both[1:2]
            volume = vol_ref[p, :, t * tvox : (t + 1) * tvox]
            sart = jnp.maximum(volume + RELAX * (sums[0] / sums[1]), 0.0)
            out_ref[p * tiles + t] = sart
            gap = sart - volume
            gap_sum += gap * gap
    out_ref[planes * tiles] = gap_sum


def back_project(plan, volume, footprint, tile_block, tile_cells, parts):
    planes, rows, tiles, views, tdet, tvox = footprint.shape
    shape = planes, rows, tiles, views, tvox, tdet
    spaces = [pl.ANY, pltpu.VMEM, pl.ANY, pl.ANY] + [pltpu.VMEM] * len(parts)
    footprint = pltpu.with_memory_space_constraint(footprint, pltpu.VMEM)
    return pl.pallas_call(
        functools.partial(back_kernel, plan, shape),
        out_shape=jax.ShapeDtypeStruct((planes * tiles + 1, rows, tvox), jnp.float32),
        in_specs=[pl.BlockSpec(memory_space=space) for space in spaces],
        out_specs=pl.BlockSpec(memory_space=pltpu.VMEM),
        scratch_shapes=[
            pltpu.VMEM((2, rows, tvox), jnp.float32),
            pltpu.VMEM((views, plan.units + plan.halo_units, plan.unit, tdet), jnp.float32),
            pltpu.VMEM(volume.shape, jnp.float32),
            pltpu.SMEM(tile_block.shape, jnp.int32),
            pltpu.SMEM(tile_cells.shape, jnp.int32),
            pltpu.SemaphoreType.DMA((3,)),
        ],
        compiler_params=pltpu.CompilerParams(vmem_limit_bytes=VMEM_BYTES // 2),
        name="back_project",
    )(volume, footprint, tile_block, tile_cells, *parts)


def unit_at_rim(cells):
    return cells * lax.rsqrt(cells * cells + SMOOTHING)


def slope_of(here, after, unit_before, size, masks):
    high, wide = size
    first_row, last_row, first_cell, last_cell = masks
    lanes = here[0, 0].shape[1]
    next_row = {k: pltpu.roll(x, 7, 0) for k, x in here.items()}
    next_cell = {k: pltpu.roll(x, lanes - 1, 1) for k, x in here.items()}
    slope, unit_a, unit_b, unit_e = {}, {}, {}, {}
    for i, t in here:
        k, x = (i, t), here[i, t]
        row = next_row[i + 1, t] if i + 1 < high else 0.0
        cell = next_cell[i, t + 1] if t + 1 < wide else 0.0
        diff_a = after[k] - x
        diff_b = jnp.where(last_row, row, next_row[k]) - x
        diff_e = jnp.where(last_cell, cell, next_cell[k]) - x
        scale = lax.rsqrt(diff_a * diff_a + diff_b * diff_b + diff_e * diff_e + SMOOTHING)
        unit_a[k], unit_b[k], unit_e[k] = diff_a * scale, diff_b * scale, diff_e * scale
        slope[k] = unit_before[k] - (diff_a + diff_b + diff_e) * scale
    past_row = {k: pltpu.roll(x, 1, 0) for k, x in unit_b.items()}
    past_cell = {k: pltpu.roll(x, 1, 1) for k, x in unit_e.items()}
    for i, t in here:
        k = (i, t)
        rim = unit_at_rim(here[k]) if i == 0 or t == 0 else None
        row = past_row[i - 1, t] if i else rim
        cell = past_cell[i, t - 1] if t else rim
        slope[k] += jnp.where(first_row, row, past_row[k])
        slope[k] += jnp.where(first_cell, cell, past_cell[k])
    return slope, unit_a


def smooth_kernel(sizes, exact_ref, *rest):
    chip_refs, (out_ref, seen_ref, field, slopes, units) = rest[:-5], rest[-5:]
    slabs, bands, planes, rows, tiles, tvox = sizes
    slab, band = lax.axis_index("slab"), lax.axis_index("xy")
    depth, per = slabs * planes, rows // 8
    size = bands * per, tiles
    blocks = [(i, t) for i in range(size[0]) for t in range(size[1])]

    views, own, unit, tdet = exact_ref.shape
    for v in range(views):
        for i in range(own):
            for c in range(unit):
                at = (i * unit + c) * tdet
                seen_ref[v : v + 1, at : at + tdet] = exact_ref[v, i, c : c + 1, :]

    gap = jnp.zeros((rows, tvox), jnp.float32)
    flips = list(range(0, slabs, 2))
    flips += [flip ^ 1 for flip in flips[::-1]]
    for flip, ref in zip(flips, chip_refs):
        for j in range(bands):
            plane, at = (slab ^ flip) * planes, (band ^ j) * per
            for p in range(planes):
                for t in range(tiles):
                    tile = ref[(j * planes + p) * tiles + t]
                    for n in range(per):
                        field[plane + p, at + n, t] = tile[8 * n : 8 * n + 8]
        gap += ref[bands * planes * tiles]
    nothing = jnp.zeros((8, tvox), jnp.float32)
    for i, t in blocks:
        field[depth, i, t] = nothing
        slopes[depth, i, t] = nothing
    row_ids = lax.broadcasted_iota(jnp.int32, (8, tvox), 0)
    cell_ids = lax.broadcasted_iota(jnp.int32, (8, tvox), 1)
    masks = (row_ids == 0, row_ids == 7, cell_ids == 0, cell_ids == tvox - 1)

    def total(square):
        return jnp.sum(jnp.sum(square, axis=0, keepdims=True), axis=1, keepdims=True)

    def finish(p, here, after, square):
        before = {(i, t): units[i, t] for i, t in blocks}
        slope, unit_a = slope_of(here, after, before, size, masks)
        for i, t in blocks:
            slopes[p, i, t] = slope[i, t]
            units[i, t] = unit_a[i, t]
            square = square + slope[i, t] * slope[i, t]
        return square

    norm = jnp.sqrt(total(gap))
    unroll = 4 if depth % 4 == 0 and len(blocks) <= 16 else 1

    def one(p, square):
        here = {(i, t): field[p, i, t] for i, t in blocks}
        after = {(i, t): field[p + 1, i, t] for i, t in blocks}
        return finish(p, here, after, square)

    for i, t in blocks:
        units[i, t] = unit_at_rim(field[0, i, t])
    square = lax.fori_loop(0, depth, one, nothing, unroll=unroll)
    step = TV_RATE * norm / jnp.sqrt(total(square) + 1e-06)

    def two(p, square):
        here = {(i, t): field[p, i, t] for i, t in blocks}
        after = {(i, t): field[p + 1, i, t] - step * slopes[p + 1, i, t] for i, t in blocks}
        for i, t in blocks:
            field[p + 1, i, t] = after[i, t]
        return finish(p, here, after, square)

    for i, t in blocks:
        here = field[0, i, t] - step * slopes[0, i, t]
        field[0, i, t] = here
        units[i, t] = unit_at_rim(here)
    square = lax.fori_loop(0, depth, two, nothing, unroll=unroll)
    step = TV_RATE * norm / jnp.sqrt(total(square) + 1e-06)
    for p in range(planes):
        for n in range(per):
            for t in range(tiles):
                at = slab * planes + p, band * per + n, t
                out_ref[p, 8 * n : 8 * n + 8, t * tvox : (t + 1) * tvox] = (
                    field[at] - step * slopes[at]
                )


def smooth(volume, chips, exact, slabs, bands, tiles):
    planes, rows, cells = volume.shape
    views, own, unit, tdet = exact.shape
    sizes = slabs, bands, planes, rows, tiles, cells // tiles
    plane = bands * rows // 8, tiles, 8, cells // tiles
    return pl.pallas_call(
        functools.partial(smooth_kernel, sizes),
        out_shape=(
            jax.ShapeDtypeStruct(volume.shape, jnp.float32),
            jax.ShapeDtypeStruct((views, own * unit * tdet), jnp.float32),
        ),
        in_specs=in_vmem(1 + len(chips)),
        out_specs=tuple(in_vmem(2)),
        scratch_shapes=[
            pltpu.VMEM((slabs * planes + 1,) + plane, jnp.float32),
            pltpu.VMEM((slabs * planes + 1,) + plane, jnp.float32),
            pltpu.VMEM(plane, jnp.float32),
        ],
        compiler_params=pltpu.CompilerParams(vmem_limit_bytes=VMEM_BYTES),
        name="smooth",
    )(exact, *chips)


def body(volume, footprint, tile_block, tile_cells, measured):
    views, tdet = footprint.shape[3], footprint.shape[5]
    slabs, bands = lax.axis_size("slab"), lax.axis_size("xy")
    plan = Plan(slabs, bands, views, measured.shape[1] // tdet, tdet)
    block, cells = (jnp.transpose(each, (0, 2, 3, 1)) for each in (tile_block, tile_cells))

    packed, low, high, seen, footprint = project(
        plan, volume, footprint, block, cells, measured
    )
    below, above = shift_all(high, "slab", 1), shift_all(low, "slab", -1)
    chunks = shares(plan, packed, below, above)
    parts = [
        swap_all(chunks[flip], "xy", flip) if flip else chunks[0] for flip in reduce_order(bands)
    ]
    turned = turn(footprint)
    exact, rounded = correct(plan, seen, parts, turned)
    parts = [rounded] + [swap_all(rounded, "xy", flip) for flip in range(1, bands)]
    tiled = back_project(plan, volume, turned, block, cells, parts)

    line = [tiled] + [swap_all(tiled, "xy", flip) for flip in range(1, bands)]
    line = jnp.concatenate([each[:-1] for each in line] + [sum(each[-1:] for each in line)])
    chips = [line] + [swap_all(line, "slab", flip) for flip in range(2, slabs, 2)]
    chips += [swap_all(each, "slab", 1) for each in chips[::-1]]
    return smooth(volume, chips, exact, slabs, bands, footprint.shape[2])


def solution(mesh):
    placed = (
        P("slab", "xy", None),
        P("slab", "xy", None, None, None, None),
        P("slab", "xy", None, None),
        P("slab", "xy", None, None),
        P(),
    )
    return jax.shard_map(
        body,
        mesh=mesh,
        in_specs=placed,
        out_specs=(P("slab", "xy", None), P(None, ("slab", "xy"))),
        check_vma=False,
    )
```

```python
import functools

import jax
import jax.numpy as jnp
from jax import lax
from jax.experimental import pallas as pl
from jax.experimental.pallas import tpu as pltpu
from jax.sharding import PartitionSpec as P

RELAX = 1.0
TV_RATE = 0.8
SMOOTHING = 0.01
DCOLS = 2048
VMEM_BYTES = 32 * 1024 * 1024


class Plan:
    def __init__(self, slabs, bands, views, nblocks, tdet):
        self.slabs, self.bands, self.views, self.tdet = slabs, bands, views, tdet
        per_row = DCOLS // tdet
        own = nblocks // (slabs * bands)
        self.slab_own = nblocks // slabs
        self.halo = per_row
        self.unit = min(per_row, own)
        self.own_units = own // self.unit
        self.halo_units = per_row // self.unit
        self.units = self.slab_own // self.unit + 2 * self.halo_units
        self.chunk = self.own_units + self.halo_units
        narrow = per_row // bands
        fits = self.unit == per_row and narrow * bands == per_row and narrow + 2 < per_row
        self.narrow = narrow if fits else 0
        self.width = [
            self.narrow + 2 if v % 2 and self.narrow else self.unit for v in range(views)
        ]
        self.base = [2 * sum(self.width[:v]) for v in range(views)]
        self.lines = 2 * sum(self.width)

    def is_narrow(self, v):
        return self.width[v] != self.unit


def shift_all(cells, axis, step):
    count = lax.axis_size(axis)
    return lax.ppermute(cells, axis, [(i, (i + step) % count) for i in range(count)])


def reduce_order(bands):
    return [0] + [flip for flip in (3, 1, 2) if flip < bands] + list(range(4, bands))


def swap_all(cells, axis, flip):
    count = lax.axis_size(axis)
    return lax.ppermute(cells, axis, [(i, i ^ flip) for i in range(count)])


def unit_of(plan, block, slab):
    local = jnp.clip(
        block - slab * plan.slab_own + plan.halo, 0, plan.units * plan.unit - 1
    )
    if plan.unit & (plan.unit - 1):
        return lax.div(local, plan.unit), lax.rem(local, plan.unit)
    return local >> (plan.unit.bit_length() - 1), local & (plan.unit - 1)


def copy_all(pairs, sems):
    return [pltpu.make_async_copy(src, dst, sems.at[n]) for n, (src, dst) in enumerate(pairs)]


def stream_spans(planes, rows):
    size = max(rows // 4, 1)
    return [(p, r, min(size, rows - r)) for p in range(planes) for r in range(0, rows, size)]


def project_kernel(
    plan, shape, vol_hbm, foot_hbm, block_hbm, cells_hbm, seen_hbm,
    out_ref, low_ref, high_ref, seen_ref, foot, acc, vol_ref, block_ref, cells_ref, seen, sems, small,
):
    planes, rows, tiles, views, tvox, tdet = shape
    slab, band = lax.axis_index("slab"), lax.axis_index("xy")
    spans = stream_spans(planes, rows)
    span = plan.unit * tdet
    own_at = (slab * plan.bands + band) * plan.own_units
    halo_at = jnp.where(
        band == 0,
        slab * (plan.slab_own // plan.unit) - plan.halo_units,
        (slab + 1) * (plan.slab_own // plan.unit),
    )
    halo_at = jnp.clip(halo_at, 0, seen_hbm.shape[1] // span - plan.halo_units)
    own_at, halo_at = (pl.multiple_of(at * span, span) for at in (own_at, halo_at))
    own_size, halo_size = plan.own_units * span, plan.halo_units * span
    first = copy_all(
        [
            (block_hbm, block_ref),
            (cells_hbm, cells_ref),
            (vol_hbm, vol_ref),
            (seen_hbm.at[:, pl.ds(own_at, own_size)], seen.at[:, pl.ds(0, own_size)]),
            (seen_hbm.at[:, pl.ds(halo_at, halo_size)], seen.at[:, pl.ds(own_size, halo_size)]),
        ],
        small,
    )
    stream = [(foot_hbm.at[p, pl.ds(r, n)], foot.at[p, pl.ds(r, n)]) for p, r, n in spans]
    stream = copy_all(stream, sems)
    for copy in first:
        copy.start()
    for copy in stream:
        copy.start(priority=1)
    acc[...] = jnp.zeros_like(acc)
    top = lax.broadcasted_iota(jnp.int32, (8, tvox), 0) == 0
    lane = lax.broadcasted_iota(jnp.int32, (8, tdet), 1)
    for copy in first:
        copy.wait()
    for v in range(views):
        for i in range(plan.chunk):
            for c in range(plan.unit):
                at = (i * plan.unit + c) * tdet
                seen_ref[v, i, c : c + 1, :] = seen[v : v + 1, at : at + tdet]
    starts = [plan.units * sum(plan.width[:v]) for v in range(views)]
    for copy, (p, begin, size) in zip(stream, spans):
        copy.wait()
        for r in range(begin, begin + size):
            for t in range(tiles):
                voxels = vol_ref[p, r : r + 1, t * tvox : (t + 1) * tvox]
                left = jnp.where(top, jnp.broadcast_to(voxels, (8, tvox)), 1.0)
                left = left.astype(jnp.bfloat16)
                for v in range(views):
                    sums = jnp.dot(left, foot[p, r, t, v], preferred_element_type=jnp.float32)
                    sums = jnp.where(lane < cells_ref[p, t, v, r], sums, 0.0)
                    unit, column = unit_of(plan, block_ref[p, t, v, r], slab)
                    if plan.is_narrow(v):
                        column = column - (band * plan.narrow - 1)
                        column = jnp.clip(column, 0, plan.width[v] - 1)
                    acc[starts[v] + unit * plan.width[v] + column] += sums
    for unit in range(plan.units):
        for v in range(views):
            width = plan.width[v]
            at = starts[v] + unit * width
            for q in range(2):
                line = plan.base[v] + q * width
                out_ref[unit, line : line + width, :] = acc[at : at + width, q, :]
    edge = 2 * plan.halo_units
    low_ref[...] = out_ref[:edge]
    high_ref[...] = out_ref[plan.units - edge :]


def in_vmem(count):
    return [pl.BlockSpec(memory_space=pltpu.VMEM)] * count


def project(plan, volume, footprint, tile_block, tile_cells, measured):
    shape = footprint.shape
    views, tdet = plan.views, plan.tdet
    parts = len(stream_spans(*shape[:2]))
    operands = [
        pltpu.with_memory_space_constraint(operand, pltpu.HBM)
        for operand in (volume, footprint, tile_block, tile_cells, measured)
    ]
    border = (2 * plan.halo_units, plan.lines, tdet)
    return pl.pallas_call(
        functools.partial(project_kernel, plan, shape),
        out_shape=(
            jax.ShapeDtypeStruct((plan.units, plan.lines, tdet), jnp.float32),
            jax.ShapeDtypeStruct(border, jnp.float32),
            jax.ShapeDtypeStruct(border, jnp.float32),
            jax.ShapeDtypeStruct((views, plan.chunk, plan.unit, tdet), jnp.float32),
            pltpu.VMEM(shape, jnp.bfloat16),
        ),
        in_specs=[pl.BlockSpec(memory_space=pltpu.HBM)] * 5,
        out_specs=tuple(in_vmem(5)),
        scratch_shapes=[
            pltpu.VMEM((plan.units * sum(plan.width), 8, tdet), jnp.float32),
            pltpu.VMEM(volume.shape, jnp.float32),
            pltpu.SMEM(tile_block.shape, jnp.int32),
            pltpu.SMEM(tile_cells.shape, jnp.int32),
            pltpu.VMEM((views, plan.chunk * plan.unit * tdet), jnp.float32),
            pltpu.SemaphoreType.DMA((parts,)),
            pltpu.SemaphoreType.DMA((5,)),
        ],
        compiler_params=pltpu.CompilerParams(vmem_limit_bytes=VMEM_BYTES),
        name="project",
    )(*operands)


def share_kernel(plan, packed_ref, below_ref, above_ref, *rest):
    out_refs, total = rest[:-1], rest[-1]
    slab, band = lax.axis_index("slab"), lax.axis_index("xy")
    edge = 2 * plan.halo_units
    total[...] = packed_ref[...]
    total[:edge] += jnp.where(slab == 0, 0.0, below_ref[...])
    total[plan.units - edge :] += jnp.where(slab == plan.slabs - 1, 0.0, above_ref[...])
    for flip, out_ref in enumerate(out_refs):
        owner = band ^ flip
        for i in range(plan.own_units):
            out_ref[i] = total[plan.halo_units + owner * plan.own_units + i]
        halo = jnp.where(owner == 0, 0, plan.units - plan.halo_units)
        for i in range(plan.halo_units):
            out_ref[plan.own_units + i] = total[halo + i]


def shares(plan, packed, below, above):
    chunk = jax.ShapeDtypeStruct((plan.chunk,) + packed.shape[1:], jnp.float32)
    return pl.pallas_call(
        functools.partial(share_kernel, plan),
        out_shape=(chunk,) * plan.bands,
        in_specs=in_vmem(3),
        out_specs=tuple(in_vmem(plan.bands)),
        scratch_shapes=[pltpu.VMEM(packed.shape, jnp.float32)],
        compiler_params=pltpu.CompilerParams(vmem_limit_bytes=VMEM_BYTES // 4),
        name="shares",
    )(packed, below, above)


def correct_kernel(plan, seen_ref, ready_ref, *rest):
    del ready_ref
    parts, (exact_ref, rounded_ref) = rest[:-2], rest[-2:]
    band = lax.axis_index("xy")
    tdet, unit = plan.tdet, plan.unit
    rounded = []
    for v in range(plan.views):
        width = plan.width[v]
        for i in range(plan.chunk):
            sums = []
            for q in range(2):
                line = plan.base[v] + q * width
                total = 0.0
                for flip, part in zip(reduce_order(plan.bands), parts):
                    piece = part[i, line : line + width, :]
                    if plan.is_narrow(v):
                        room = jnp.zeros((unit - width, tdet), jnp.float32)
                        piece = jnp.concatenate([piece, room], axis=0)
                        first = (band ^ flip) * plan.narrow - 1
                        piece = pltpu.roll(piece, lax.rem(first + unit, unit), 0)
                    total = total + piece
                sums.append(total)
            corrected = (seen_ref[v, i] - sums[0]) / jnp.maximum(sums[1], 1.0)
            rounded.append(corrected)
            if i < plan.own_units:
                exact_ref[v, i] = corrected
    rounded_ref[...] = jnp.concatenate(rounded, axis=0).astype(jnp.bfloat16)


def correct(plan, seen, parts, ready):
    views, chunk, unit, tdet = seen.shape
    return pl.pallas_call(
        functools.partial(correct_kernel, plan),
        out_shape=(
            jax.ShapeDtypeStruct((views, plan.own_units, unit, tdet), jnp.float32),
            jax.ShapeDtypeStruct((views * chunk * unit, tdet), jnp.bfloat16),
        ),
        in_specs=in_vmem(1) + [pl.BlockSpec(memory_space=pl.ANY)] + in_vmem(len(parts)),
        out_specs=tuple(in_vmem(2)),
        compiler_params=pltpu.CompilerParams(vmem_limit_bytes=VMEM_BYTES // 4),
        name="correct",
    )(seen, ready, *parts)


def turn_kernel(shape, foot, turned):
    for p in range(shape[0]):
        for r in range(shape[1]):
            for t in range(shape[2]):
                for v in range(shape[3]):
                    turned[p, r, t, v] = foot[p, r, t, v].T


def turn(footprint):
    shape = footprint.shape
    footprint = pltpu.with_memory_space_constraint(footprint, pltpu.VMEM)
    return pl.pallas_call(
        functools.partial(turn_kernel, shape),
        out_shape=pltpu.VMEM(shape[:4] + (shape[5], shape[4]), jnp.bfloat16),
        in_specs=in_vmem(1),
        out_specs=pl.BlockSpec(memory_space=pltpu.VMEM),
        compiler_params=pltpu.CompilerParams(vmem_limit_bytes=VMEM_BYTES // 4),
        cost_estimate=pl.CostEstimate(
            flops=0, bytes_accessed=4 * footprint.size, transcendentals=0
        ),
        name="turn",
    )(footprint)


def back_kernel(plan, shape, vol_any, foot, block_any, cells_any, *rest):
    parts, (out_ref, sums, corr, vol_ref, block_ref, cells_ref, small) = rest[:-7], rest[-7:]
    planes, rows, tiles, views, tvox, tdet = shape
    slab, band = lax.axis_index("slab"), lax.axis_index("xy")
    first = copy_all([(block_any, block_ref), (cells_any, cells_ref), (vol_any, vol_ref)], small)
    for copy in first:
        copy.start()
    for flip, part in enumerate(parts):
        source = band ^ flip
        piece = part[...].astype(jnp.float32).reshape(views, plan.chunk, plan.unit, tdet)
        halo = jnp.where(
            source == 0,
            0,
            jnp.where(source == plan.bands - 1, plan.units - plan.halo_units, plan.units),
        )
        for v in range(views):
            for i in range(plan.own_units):
                corr[v, plan.halo_units + source * plan.own_units + i] = piece[v, i]
            for i in range(plan.halo_units):
                corr[v, halo + i] = piece[v, plan.own_units + i]
    top = lax.broadcasted_iota(jnp.int32, (8, tdet), 0) == 0
    lane = lax.broadcasted_iota(jnp.int32, (8, tdet), 1)
    for copy in first:
        copy.wait()
    gap_sum = jnp.zeros((rows, tvox), jnp.float32)
    for p in range(planes):
        for t in range(tiles):
            for r in range(rows):
                lefts = []
                for v in range(views):
                    unit, column = unit_of(plan, block_ref[p, t, v, r], slab)
                    picked = jnp.broadcast_to(corr[v, unit, pl.ds(column, 1), :], (8, tdet))
                    left = jnp.where(top, picked, 1.0)
                    left = jnp.where(lane < cells_ref[p, t, v, r], left, 0.0)
                    lefts.append(left.astype(jnp.bfloat16))
                both = jnp.dot(
                    jnp.concatenate(lefts, axis=1),
                    foot[p, r, t].reshape(views * tdet, tvox),
                    preferred_element_type=jnp.float32,
                )
                sums[0, r : r + 1] = both[0:1]
                sums[1, r : r + 1] = both[1:2]
            volume = vol_ref[p, :, t * tvox : (t + 1) * tvox]
            sart = jnp.maximum(volume + RELAX * (sums[0] / sums[1]), 0.0)
            out_ref[p * tiles + t] = sart
            gap = sart - volume
            gap_sum += gap * gap
    out_ref[planes * tiles] = gap_sum


def back_project(plan, volume, footprint, tile_block, tile_cells, parts):
    planes, rows, tiles, views, tdet, tvox = footprint.shape
    shape = planes, rows, tiles, views, tvox, tdet
    spaces = [pl.ANY, pltpu.VMEM, pl.ANY, pl.ANY] + [pltpu.VMEM] * len(parts)
    footprint = pltpu.with_memory_space_constraint(footprint, pltpu.VMEM)
    return pl.pallas_call(
        functools.partial(back_kernel, plan, shape),
        out_shape=jax.ShapeDtypeStruct((planes * tiles + 1, rows, tvox), jnp.float32),
        in_specs=[pl.BlockSpec(memory_space=space) for space in spaces],
        out_specs=pl.BlockSpec(memory_space=pltpu.VMEM),
        scratch_shapes=[
            pltpu.VMEM((2, rows, tvox), jnp.float32),
            pltpu.VMEM((views, plan.units + plan.halo_units, plan.unit, tdet), jnp.float32),
            pltpu.VMEM(volume.shape, jnp.float32),
            pltpu.SMEM(tile_block.shape, jnp.int32),
            pltpu.SMEM(tile_cells.shape, jnp.int32),
            pltpu.SemaphoreType.DMA((3,)),
        ],
        compiler_params=pltpu.CompilerParams(vmem_limit_bytes=VMEM_BYTES // 2),
        name="back_project",
    )(volume, footprint, tile_block, tile_cells, *parts)


def unit_at_rim(cells):
    return cells * lax.rsqrt(cells * cells + SMOOTHING)


def slope_of(here, after, unit_before, size, masks):
    high, wide = size
    first_row, last_row, first_cell, last_cell = masks
    lanes = here[0, 0].shape[1]
    next_row = {k: pltpu.roll(x, 7, 0) for k, x in here.items()}
    next_cell = {k: pltpu.roll(x, lanes - 1, 1) for k, x in here.items()}
    slope, unit_a, unit_b, unit_e = {}, {}, {}, {}
    for i, t in here:
        k, x = (i, t), here[i, t]
        row = next_row[i + 1, t] if i + 1 < high else 0.0
        cell = next_cell[i, t + 1] if t + 1 < wide else 0.0
        diff_a = after[k] - x
        diff_b = jnp.where(last_row, row, next_row[k]) - x
        diff_e = jnp.where(last_cell, cell, next_cell[k]) - x
        scale = lax.rsqrt(diff_a * diff_a + diff_b * diff_b + diff_e * diff_e + SMOOTHING)
        unit_a[k], unit_b[k], unit_e[k] = diff_a * scale, diff_b * scale, diff_e * scale
        slope[k] = unit_before[k] - (diff_a + diff_b + diff_e) * scale
    past_row = {k: pltpu.roll(x, 1, 0) for k, x in unit_b.items()}
    past_cell = {k: pltpu.roll(x, 1, 1) for k, x in unit_e.items()}
    for i, t in here:
        k = (i, t)
        rim = unit_at_rim(here[k]) if i == 0 or t == 0 else None
        row = past_row[i - 1, t] if i else rim
        cell = past_cell[i, t - 1] if t else rim
        slope[k] += jnp.where(first_row, row, past_row[k])
        slope[k] += jnp.where(first_cell, cell, past_cell[k])
    return slope, unit_a


def smooth_kernel(sizes, exact_ref, *rest):
    chip_refs, (out_ref, seen_ref, field, slopes, units) = rest[:-5], rest[-5:]
    slabs, bands, planes, rows, tiles, tvox = sizes
    slab, band = lax.axis_index("slab"), lax.axis_index("xy")
    depth, per = slabs * planes, rows // 8
    size = bands * per, tiles
    blocks = [(i, t) for i in range(size[0]) for t in range(size[1])]

    views, own, unit, tdet = exact_ref.shape
    for v in range(views):
        for i in range(own):
            for c in range(unit):
                at = (i * unit + c) * tdet
                seen_ref[v : v + 1, at : at + tdet] = exact_ref[v, i, c : c + 1, :]

    gap = jnp.zeros((rows, tvox), jnp.float32)
    flips = list(range(0, slabs, 2))
    flips += [flip ^ 1 for flip in flips[::-1]]
    for flip, ref in zip(flips, chip_refs):
        for j in range(bands):
            plane, at = (slab ^ flip) * planes, (band ^ j) * per
            for p in range(planes):
                for t in range(tiles):
                    tile = ref[(j * planes + p) * tiles + t]
                    for n in range(per):
                        field[plane + p, at + n, t] = tile[8 * n : 8 * n + 8]
        gap += ref[bands * planes * tiles]
    nothing = jnp.zeros((8, tvox), jnp.float32)
    for i, t in blocks:
        field[depth, i, t] = nothing
        slopes[depth, i, t] = nothing
    row_ids = lax.broadcasted_iota(jnp.int32, (8, tvox), 0)
    cell_ids = lax.broadcasted_iota(jnp.int32, (8, tvox), 1)
    masks = (row_ids == 0, row_ids == 7, cell_ids == 0, cell_ids == tvox - 1)

    def total(square):
        return jnp.sum(jnp.sum(square, axis=0, keepdims=True), axis=1, keepdims=True)

    def finish(p, here, after, square):
        before = {(i, t): units[i, t] for i, t in blocks}
        slope, unit_a = slope_of(here, after, before, size, masks)
        for i, t in blocks:
            slopes[p, i, t] = slope[i, t]
            units[i, t] = unit_a[i, t]
            square = square + slope[i, t] * slope[i, t]
        return square

    norm = jnp.sqrt(total(gap))
    unroll = 4 if depth % 4 == 0 and len(blocks) <= 16 else 1

    def one(p, square):
        here = {(i, t): field[p, i, t] for i, t in blocks}
        after = {(i, t): field[p + 1, i, t] for i, t in blocks}
        return finish(p, here, after, square)

    for i, t in blocks:
        units[i, t] = unit_at_rim(field[0, i, t])
    square = lax.fori_loop(0, depth, one, nothing, unroll=unroll)
    step = TV_RATE * norm / jnp.sqrt(total(square) + 1e-06)

    def two(p, square):
        here = {(i, t): field[p, i, t] for i, t in blocks}
        after = {(i, t): field[p + 1, i, t] - step * slopes[p + 1, i, t] for i, t in blocks}
        for i, t in blocks:
            field[p + 1, i, t] = after[i, t]
        return finish(p, here, after, square)

    for i, t in blocks:
        here = field[0, i, t] - step * slopes[0, i, t]
        field[0, i, t] = here
        units[i, t] = unit_at_rim(here)
    square = lax.fori_loop(0, depth, two, nothing, unroll=unroll)
    step = TV_RATE * norm / jnp.sqrt(total(square) + 1e-06)
    for p in range(planes):
        for n in range(per):
            for t in range(tiles):
                at = slab * planes + p, band * per + n, t
                out_ref[p, 8 * n : 8 * n + 8, t * tvox : (t + 1) * tvox] = (
                    field[at] - step * slopes[at]
                )


def smooth(volume, chips, exact, slabs, bands, tiles):
    planes, rows, cells = volume.shape
    views, own, unit, tdet = exact.shape
    sizes = slabs, bands, planes, rows, tiles, cells // tiles
    plane = bands * rows // 8, tiles, 8, cells // tiles
    return pl.pallas_call(
        functools.partial(smooth_kernel, sizes),
        out_shape=(
            jax.ShapeDtypeStruct(volume.shape, jnp.float32),
            jax.ShapeDtypeStruct((views, own * unit * tdet), jnp.float32),
        ),
        in_specs=in_vmem(1 + len(chips)),
        out_specs=tuple(in_vmem(2)),
        scratch_shapes=[
            pltpu.VMEM((slabs * planes + 1,) + plane, jnp.float32),
            pltpu.VMEM((slabs * planes + 1,) + plane, jnp.float32),
            pltpu.VMEM(plane, jnp.float32),
        ],
        compiler_params=pltpu.CompilerParams(vmem_limit_bytes=VMEM_BYTES),
        name="smooth",
    )(exact, *chips)


def body(volume, footprint, tile_block, tile_cells, measured):
    views, tdet = footprint.shape[3], footprint.shape[5]
    slabs, bands = lax.axis_size("slab"), lax.axis_size("xy")
    plan = Plan(slabs, bands, views, measured.shape[1] // tdet, tdet)
    block, cells = (jnp.transpose(each, (0, 2, 3, 1)) for each in (tile_block, tile_cells))

    packed, low, high, seen, footprint = project(
        plan, volume, footprint, block, cells, measured
    )
    below, above = shift_all(high, "slab", 1), shift_all(low, "slab", -1)
    chunks = shares(plan, packed, below, above)
    parts = [
        swap_all(chunks[flip], "xy", flip) if flip else chunks[0] for flip in reduce_order(bands)
    ]
    turned = turn(footprint)
    exact, rounded = correct(plan, seen, parts, turned)
    parts = [rounded] + [swap_all(rounded, "xy", flip) for flip in range(1, bands)]
    tiled = back_project(plan, volume, turned, block, cells, parts)

    line = [tiled] + [swap_all(tiled, "xy", flip) for flip in range(1, bands)]
    line = jnp.concatenate([each[:-1] for each in line] + [sum(each[-1:] for each in line)])
    chips = [line] + [swap_all(line, "slab", flip) for flip in range(2, slabs, 2)]
    chips += [swap_all(each, "slab", 1) for each in chips[::-1]]
    return smooth(volume, chips, exact, slabs, bands, footprint.shape[2])


def solution(mesh):
    placed = (
        P("slab", "xy", None),
        P("slab", "xy", None, None, None, None),
        P("slab", "xy", None, None),
        P("slab", "xy", None, None),
        P(),
    )
    return jax.shard_map(
        body,
        mesh=mesh,
        in_specs=placed,
        out_specs=(P("slab", "xy", None), P(None, ("slab", "xy"))),
        check_vma=False,
    )
```

```python
import functools

import jax
import jax.numpy as jnp
from jax import lax
from jax.experimental import pallas as pl
from jax.experimental.pallas import tpu as pltpu
from jax.sharding import PartitionSpec as P

RELAX = 1.0
TV_RATE = 0.8
SMOOTHING = 0.01
DCOLS = 2048
VMEM_BYTES = 32 * 1024 * 1024


class Plan:
    def __init__(self, slabs, bands, views, nblocks, tdet):
        self.slabs, self.bands, self.views, self.tdet = slabs, bands, views, tdet
        per_row = DCOLS // tdet
        own = nblocks // (slabs * bands)
        self.slab_own = nblocks // slabs
        self.halo = per_row
        self.unit = min(per_row, own)
        self.own_units = own // self.unit
        self.halo_units = per_row // self.unit
        self.units = self.slab_own // self.unit + 2 * self.halo_units
        self.chunk = self.own_units + self.halo_units
        narrow = per_row // bands
        fits = self.unit == per_row and narrow * bands == per_row and narrow + 2 < per_row
        self.narrow = narrow if fits else 0
        self.width = [
            self.narrow + 2 if v % 2 and self.narrow else self.unit for v in range(views)
        ]
        self.base = [2 * sum(self.width[:v]) for v in range(views)]
        self.lines = 2 * sum(self.width)

    def is_narrow(self, v):
        return self.width[v] != self.unit


def shift_all(cells, axis, step):
    count = lax.axis_size(axis)
    return lax.ppermute(cells, axis, [(i, (i + step) % count) for i in range(count)])


def reduce_order(bands):
    return [0] + [flip for flip in (3, 1, 2) if flip < bands] + list(range(4, bands))


def swap_all(cells, axis, flip):
    count = lax.axis_size(axis)
    return lax.ppermute(cells, axis, [(i, i ^ flip) for i in range(count)])


def unit_of(plan, block, slab):
    local = jnp.clip(
        block - slab * plan.slab_own + plan.halo, 0, plan.units * plan.unit - 1
    )
    if plan.unit & (plan.unit - 1):
        return lax.div(local, plan.unit), lax.rem(local, plan.unit)
    return local >> (plan.unit.bit_length() - 1), local & (plan.unit - 1)


def copy_all(pairs, sems):
    return [pltpu.make_async_copy(src, dst, sems.at[n]) for n, (src, dst) in enumerate(pairs)]


def stream_spans(planes, rows):
    size = max(rows // 4, 1)
    return [(p, r, min(size, rows - r)) for p in range(planes) for r in range(0, rows, size)]


def project_kernel(
    plan, shape, vol_hbm, foot_hbm, block_hbm, cells_hbm, seen_hbm,
    out_ref, low_ref, high_ref, seen_ref, foot, acc, vol_ref, block_ref, cells_ref, seen, sems, small,
):
    planes, rows, tiles, views, tvox, tdet = shape
    slab, band = lax.axis_index("slab"), lax.axis_index("xy")
    spans = stream_spans(planes, rows)
    span = plan.unit * tdet
    own_at = (slab * plan.bands + band) * plan.own_units
    halo_at = jnp.where(
        band == 0,
        slab * (plan.slab_own // plan.unit) - plan.halo_units,
        (slab + 1) * (plan.slab_own // plan.unit),
    )
    halo_at = jnp.clip(halo_at, 0, seen_hbm.shape[1] // span - plan.halo_units)
    own_at, halo_at = (pl.multiple_of(at * span, span) for at in (own_at, halo_at))
    own_size, halo_size = plan.own_units * span, plan.halo_units * span
    first = copy_all(
        [
            (block_hbm, block_ref),
            (cells_hbm, cells_ref),
            (vol_hbm, vol_ref),
            (seen_hbm.at[:, pl.ds(own_at, own_size)], seen.at[:, pl.ds(0, own_size)]),
            (seen_hbm.at[:, pl.ds(halo_at, halo_size)], seen.at[:, pl.ds(own_size, halo_size)]),
        ],
        small,
    )
    stream = [(foot_hbm.at[p, pl.ds(r, n)], foot.at[p, pl.ds(r, n)]) for p, r, n in spans]
    stream = copy_all(stream, sems)
    for copy in first:
        copy.start()
    for copy in stream:
        copy.start(priority=1)
    acc[...] = jnp.zeros_like(acc)
    top = lax.broadcasted_iota(jnp.int32, (8, tvox), 0) == 0
    lane = lax.broadcasted_iota(jnp.int32, (8, tdet), 1)
    for copy in first:
        copy.wait()
    for v in range(views):
        for i in range(plan.chunk):
            for c in range(plan.unit):
                at = (i * plan.unit + c) * tdet
                seen_ref[v, i, c : c + 1, :] = seen[v : v + 1, at : at + tdet]
    starts = [plan.units * sum(plan.width[:v]) for v in range(views)]
    for copy, (p, begin, size) in zip(stream, spans):
        copy.wait()
        for r in range(begin, begin + size):
            for t in range(tiles):
                voxels = vol_ref[p, r : r + 1, t * tvox : (t + 1) * tvox]
                left = jnp.where(top, jnp.broadcast_to(voxels, (8, tvox)), 1.0)
                left = left.astype(jnp.bfloat16)
                for v in range(views):
                    sums = jnp.dot(left, foot[p, r, t, v], preferred_element_type=jnp.float32)
                    sums = jnp.where(lane < cells_ref[p, t, v, r], sums, 0.0)
                    unit, column = unit_of(plan, block_ref[p, t, v, r], slab)
                    if plan.is_narrow(v):
                        column = column - (band * plan.narrow - 1)
                        column = jnp.clip(column, 0, plan.width[v] - 1)
                    acc[starts[v] + unit * plan.width[v] + column] += sums
    for unit in range(plan.units):
        for v in range(views):
            width = plan.width[v]
            at = starts[v] + unit * width
            for q in range(2):
                line = plan.base[v] + q * width
                out_ref[unit, line : line + width, :] = acc[at : at + width, q, :]
    edge = 2 * plan.halo_units
    low_ref[...] = out_ref[:edge]
    high_ref[...] = out_ref[plan.units - edge :]


def in_vmem(count):
    return [pl.BlockSpec(memory_space=pltpu.VMEM)] * count


def project(plan, volume, footprint, tile_block, tile_cells, measured):
    shape = footprint.shape
    views, tdet = plan.views, plan.tdet
    parts = len(stream_spans(*shape[:2]))
    operands = [
        pltpu.with_memory_space_constraint(operand, pltpu.HBM)
        for operand in (volume, footprint, tile_block, tile_cells, measured)
    ]
    border = (2 * plan.halo_units, plan.lines, tdet)
    return pl.pallas_call(
        functools.partial(project_kernel, plan, shape),
        out_shape=(
            jax.ShapeDtypeStruct((plan.units, plan.lines, tdet), jnp.float32),
            jax.ShapeDtypeStruct(border, jnp.float32),
            jax.ShapeDtypeStruct(border, jnp.float32),
            jax.ShapeDtypeStruct((views, plan.chunk, plan.unit, tdet), jnp.float32),
            pltpu.VMEM(shape, jnp.bfloat16),
        ),
        in_specs=[pl.BlockSpec(memory_space=pltpu.HBM)] * 5,
        out_specs=tuple(in_vmem(5)),
        scratch_shapes=[
            pltpu.VMEM((plan.units * sum(plan.width), 8, tdet), jnp.float32),
            pltpu.VMEM(volume.shape, jnp.float32),
            pltpu.SMEM(tile_block.shape, jnp.int32),
            pltpu.SMEM(tile_cells.shape, jnp.int32),
            pltpu.VMEM((views, plan.chunk * plan.unit * tdet), jnp.float32),
            pltpu.SemaphoreType.DMA((parts,)),
            pltpu.SemaphoreType.DMA((5,)),
        ],
        compiler_params=pltpu.CompilerParams(vmem_limit_bytes=VMEM_BYTES),
        name="project",
    )(*operands)


def share_kernel(plan, packed_ref, below_ref, above_ref, *rest):
    out_refs, total = rest[:-1], rest[-1]
    slab, band = lax.axis_index("slab"), lax.axis_index("xy")
    edge = 2 * plan.halo_units
    total[...] = packed_ref[...]
    total[:edge] += jnp.where(slab == 0, 0.0, below_ref[...])
    total[plan.units - edge :] += jnp.where(slab == plan.slabs - 1, 0.0, above_ref[...])
    for flip, out_ref in enumerate(out_refs):
        owner = band ^ flip
        for i in range(plan.own_units):
            out_ref[i] = total[plan.halo_units + owner * plan.own_units + i]
        halo = jnp.where(owner == 0, 0, plan.units - plan.halo_units)
        for i in range(plan.halo_units):
            out_ref[plan.own_units + i] = total[halo + i]


def shares(plan, packed, below, above):
    chunk = jax.ShapeDtypeStruct((plan.chunk,) + packed.shape[1:], jnp.float32)
    return pl.pallas_call(
        functools.partial(share_kernel, plan),
        out_shape=(chunk,) * plan.bands,
        in_specs=in_vmem(3),
        out_specs=tuple(in_vmem(plan.bands)),
        scratch_shapes=[pltpu.VMEM(packed.shape, jnp.float32)],
        compiler_params=pltpu.CompilerParams(vmem_limit_bytes=VMEM_BYTES // 4),
        name="shares",
    )(packed, below, above)


def correct_kernel(plan, seen_ref, ready_ref, *rest):
    del ready_ref
    parts, (exact_ref, rounded_ref) = rest[:-2], rest[-2:]
    band = lax.axis_index("xy")
    tdet, unit = plan.tdet, plan.unit
    rounded = []
    for v in range(plan.views):
        width = plan.width[v]
        for i in range(plan.chunk):
            sums = []
            for q in range(2):
                line = plan.base[v] + q * width
                total = 0.0
                for flip, part in zip(reduce_order(plan.bands), parts):
                    piece = part[i, line : line + width, :]
                    if plan.is_narrow(v):
                        room = jnp.zeros((unit - width, tdet), jnp.float32)
                        piece = jnp.concatenate([piece, room], axis=0)
                        first = (band ^ flip) * plan.narrow - 1
                        piece = pltpu.roll(piece, lax.rem(first + unit, unit), 0)
                    total = total + piece
                sums.append(total)
            corrected = (seen_ref[v, i] - sums[0]) / jnp.maximum(sums[1], 1.0)
            rounded.append(corrected)
            if i < plan.own_units:
                exact_ref[v, i] = corrected
    rounded_ref[...] = jnp.concatenate(rounded, axis=0).astype(jnp.bfloat16)


def correct(plan, seen, parts, ready):
    views, chunk, unit, tdet = seen.shape
    return pl.pallas_call(
        functools.partial(correct_kernel, plan),
        out_shape=(
            jax.ShapeDtypeStruct((views, plan.own_units, unit, tdet), jnp.float32),
            jax.ShapeDtypeStruct((views * chunk * unit, tdet), jnp.bfloat16),
        ),
        in_specs=in_vmem(1) + [pl.BlockSpec(memory_space=pl.ANY)] + in_vmem(len(parts)),
        out_specs=tuple(in_vmem(2)),
        compiler_params=pltpu.CompilerParams(vmem_limit_bytes=VMEM_BYTES // 4),
        name="correct",
    )(seen, ready, *parts)


def turn_kernel(shape, foot, turned):
    for p in range(shape[0]):
        for r in range(shape[1]):
            for t in range(shape[2]):
                for v in range(shape[3]):
                    turned[p, r, t, v] = foot[p, r, t, v].T


def turn(footprint):
    shape = footprint.shape
    footprint = pltpu.with_memory_space_constraint(footprint, pltpu.VMEM)
    return pl.pallas_call(
        functools.partial(turn_kernel, shape),
        out_shape=pltpu.VMEM(shape[:4] + (shape[5], shape[4]), jnp.bfloat16),
        in_specs=in_vmem(1),
        out_specs=pl.BlockSpec(memory_space=pltpu.VMEM),
        compiler_params=pltpu.CompilerParams(vmem_limit_bytes=VMEM_BYTES // 4),
        cost_estimate=pl.CostEstimate(
            flops=0, bytes_accessed=4 * footprint.size, transcendentals=0
        ),
        name="turn",
    )(footprint)


def back_kernel(plan, shape, vol_ref, foot, block_any, cells_any, *rest):
    parts, (out_ref, sums, corr, block_ref, cells_ref, small) = rest[:-6], rest[-6:]
    planes, rows, tiles, views, tvox, tdet = shape
    slab, band = lax.axis_index("slab"), lax.axis_index("xy")
    first = copy_all([(block_any, block_ref), (cells_any, cells_ref)], small)
    for copy in first:
        copy.start()
    for flip, part in enumerate(parts):
        source = band ^ flip
        piece = part[...].astype(jnp.float32).reshape(views, plan.chunk, plan.unit, tdet)
        halo = jnp.where(
            source == 0,
            0,
            jnp.where(source == plan.bands - 1, plan.units - plan.halo_units, plan.units),
        )
        for v in range(views):
            for i in range(plan.own_units):
                corr[v, plan.halo_units + source * plan.own_units + i] = piece[v, i]
            for i in range(plan.halo_units):
                corr[v, halo + i] = piece[v, plan.own_units + i]
    top = lax.broadcasted_iota(jnp.int32, (8, tdet), 0) == 0
    lane = lax.broadcasted_iota(jnp.int32, (8, tdet), 1)
    for copy in first:
        copy.wait()
    gap_sum = jnp.zeros((rows, tvox), jnp.float32)
    for p in range(planes):
        for t in range(tiles):
            for r in range(rows):
                lefts = []
                for v in range(views):
                    unit, column = unit_of(plan, block_ref[p, t, v, r], slab)
                    picked = jnp.broadcast_to(corr[v, unit, pl.ds(column, 1), :], (8, tdet))
                    left = jnp.where(top, picked, 1.0)
                    left = jnp.where(lane < cells_ref[p, t, v, r], left, 0.0)
                    lefts.append(left.astype(jnp.bfloat16))
                both = jnp.dot(
                    jnp.concatenate(lefts, axis=1),
                    foot[p, r, t].reshape(views * tdet, tvox),
                    preferred_element_type=jnp.float32,
                )
                sums[0, r : r + 1] = both[0:1]
                sums[1, r : r + 1] = both[1:2]
            volume = vol_ref[p, :, t * tvox : (t + 1) * tvox]
            sart = jnp.maximum(volume + RELAX * (sums[0] / sums[1]), 0.0)
            out_ref[p * tiles + t] = sart
            gap = sart - volume
            gap_sum += gap * gap
    out_ref[planes * tiles] = gap_sum


def back_project(plan, volume, footprint, tile_block, tile_cells, parts):
    planes, rows, tiles, views, tdet, tvox = footprint.shape
    shape = planes, rows, tiles, views, tvox, tdet
    spaces = [pltpu.VMEM, pltpu.VMEM, pl.ANY, pl.ANY] + [pltpu.VMEM] * len(parts)
    footprint = pltpu.with_memory_space_constraint(footprint, pltpu.VMEM)
    return pl.pallas_call(
        functools.partial(back_kernel, plan, shape),
        out_shape=jax.ShapeDtypeStruct((planes * tiles + 1, rows, tvox), jnp.float32),
        in_specs=[pl.BlockSpec(memory_space=space) for space in spaces],
        out_specs=pl.BlockSpec(memory_space=pltpu.VMEM),
        scratch_shapes=[
            pltpu.VMEM((2, rows, tvox), jnp.float32),
            pltpu.VMEM((views, plan.units + plan.halo_units, plan.unit, tdet), jnp.float32),
            pltpu.SMEM(tile_block.shape, jnp.int32),
            pltpu.SMEM(tile_cells.shape, jnp.int32),
            pltpu.SemaphoreType.DMA((2,)),
        ],
        compiler_params=pltpu.CompilerParams(vmem_limit_bytes=VMEM_BYTES // 2),
        name="back_project",
    )(volume, footprint, tile_block, tile_cells, *parts)


def unit_at_rim(cells):
    return cells * lax.rsqrt(cells * cells + SMOOTHING)


def slope_of(here, after, unit_before, size, masks):
    high, wide = size
    first_row, last_row, first_cell, last_cell = masks
    lanes = here[0, 0].shape[1]
    next_row = {k: pltpu.roll(x, 7, 0) for k, x in here.items()}
    next_cell = {k: pltpu.roll(x, lanes - 1, 1) for k, x in here.items()}
    slope, unit_a, unit_b, unit_e = {}, {}, {}, {}
    for i, t in here:
        k, x = (i, t), here[i, t]
        row = next_row[i + 1, t] if i + 1 < high else 0.0
        cell = next_cell[i, t + 1] if t + 1 < wide else 0.0
        diff_a = after[k] - x
        diff_b = jnp.where(last_row, row, next_row[k]) - x
        diff_e = jnp.where(last_cell, cell, next_cell[k]) - x
        scale = lax.rsqrt(diff_a * diff_a + diff_b * diff_b + diff_e * diff_e + SMOOTHING)
        unit_a[k], unit_b[k], unit_e[k] = diff_a * scale, diff_b * scale, diff_e * scale
        slope[k] = unit_before[k] - (diff_a + diff_b + diff_e) * scale
    past_row = {k: pltpu.roll(x, 1, 0) for k, x in unit_b.items()}
    past_cell = {k: pltpu.roll(x, 1, 1) for k, x in unit_e.items()}
    for i, t in here:
        k = (i, t)
        rim = unit_at_rim(here[k]) if i == 0 or t == 0 else None
        row = past_row[i - 1, t] if i else rim
        cell = past_cell[i, t - 1] if t else rim
        slope[k] += jnp.where(first_row, row, past_row[k])
        slope[k] += jnp.where(first_cell, cell, past_cell[k])
    return slope, unit_a


def smooth_kernel(sizes, exact_ref, *rest):
    chip_refs, (out_ref, seen_ref, field, slopes, units) = rest[:-5], rest[-5:]
    slabs, bands, planes, rows, tiles, tvox = sizes
    slab, band = lax.axis_index("slab"), lax.axis_index("xy")
    depth, per = slabs * planes, rows // 8
    size = bands * per, tiles
    blocks = [(i, t) for i in range(size[0]) for t in range(size[1])]

    views, own, unit, tdet = exact_ref.shape
    for v in range(views):
        for i in range(own):
            for c in range(unit):
                at = (i * unit + c) * tdet
                seen_ref[v : v + 1, at : at + tdet] = exact_ref[v, i, c : c + 1, :]

    gap = jnp.zeros((rows, tvox), jnp.float32)
    flips = list(range(0, slabs, 2))
    flips += [flip ^ 1 for flip in flips[::-1]]
    for flip, ref in zip(flips, chip_refs):
        for j in range(bands):
            plane, at = (slab ^ flip) * planes, (band ^ j) * per
            for p in range(planes):
                for t in range(tiles):
                    tile = ref[(j * planes + p) * tiles + t]
                    for n in range(per):
                        field[plane + p, at + n, t] = tile[8 * n : 8 * n + 8]
        gap += ref[bands * planes * tiles]
    nothing = jnp.zeros((8, tvox), jnp.float32)
    for i, t in blocks:
        field[depth, i, t] = nothing
        slopes[depth, i, t] = nothing
    row_ids = lax.broadcasted_iota(jnp.int32, (8, tvox), 0)
    cell_ids = lax.broadcasted_iota(jnp.int32, (8, tvox), 1)
    masks = (row_ids == 0, row_ids == 7, cell_ids == 0, cell_ids == tvox - 1)

    def total(square):
        return jnp.sum(jnp.sum(square, axis=0, keepdims=True), axis=1, keepdims=True)

    def finish(p, here, after, square):
        before = {(i, t): units[i, t] for i, t in blocks}
        slope, unit_a = slope_of(here, after, before, size, masks)
        for i, t in blocks:
            slopes[p, i, t] = slope[i, t]
            units[i, t] = unit_a[i, t]
            square = square + slope[i, t] * slope[i, t]
        return square

    norm = jnp.sqrt(total(gap))
    unroll = 4 if depth % 4 == 0 and len(blocks) <= 16 else 1

    def one(p, square):
        here = {(i, t): field[p, i, t] for i, t in blocks}
        after = {(i, t): field[p + 1, i, t] for i, t in blocks}
        return finish(p, here, after, square)

    for i, t in blocks:
        units[i, t] = unit_at_rim(field[0, i, t])
    square = lax.fori_loop(0, depth, one, nothing, unroll=unroll)
    step = TV_RATE * norm / jnp.sqrt(total(square) + 1e-06)

    def two(p, square):
        here = {(i, t): field[p, i, t] for i, t in blocks}
        after = {(i, t): field[p + 1, i, t] - step * slopes[p + 1, i, t] for i, t in blocks}
        for i, t in blocks:
            field[p + 1, i, t] = after[i, t]
        return finish(p, here, after, square)

    for i, t in blocks:
        here = field[0, i, t] - step * slopes[0, i, t]
        field[0, i, t] = here
        units[i, t] = unit_at_rim(here)
    square = lax.fori_loop(0, depth, two, nothing, unroll=unroll)
    step = TV_RATE * norm / jnp.sqrt(total(square) + 1e-06)
    for p in range(planes):
        for n in range(per):
            for t in range(tiles):
                at = slab * planes + p, band * per + n, t
                out_ref[p, 8 * n : 8 * n + 8, t * tvox : (t + 1) * tvox] = (
                    field[at] - step * slopes[at]
                )


def smooth(volume, chips, exact, slabs, bands, tiles):
    planes, rows, cells = volume.shape
    views, own, unit, tdet = exact.shape
    sizes = slabs, bands, planes, rows, tiles, cells // tiles
    plane = bands * rows // 8, tiles, 8, cells // tiles
    return pl.pallas_call(
        functools.partial(smooth_kernel, sizes),
        out_shape=(
            jax.ShapeDtypeStruct(volume.shape, jnp.float32),
            jax.ShapeDtypeStruct((views, own * unit * tdet), jnp.float32),
        ),
        in_specs=in_vmem(1 + len(chips)),
        out_specs=tuple(in_vmem(2)),
        scratch_shapes=[
            pltpu.VMEM((slabs * planes + 1,) + plane, jnp.float32),
            pltpu.VMEM((slabs * planes + 1,) + plane, jnp.float32),
            pltpu.VMEM(plane, jnp.float32),
        ],
        compiler_params=pltpu.CompilerParams(vmem_limit_bytes=VMEM_BYTES),
        name="smooth",
    )(exact, *chips)


def body(volume, footprint, tile_block, tile_cells, measured):
    views, tdet = footprint.shape[3], footprint.shape[5]
    slabs, bands = lax.axis_size("slab"), lax.axis_size("xy")
    plan = Plan(slabs, bands, views, measured.shape[1] // tdet, tdet)
    block, cells = (jnp.transpose(each, (0, 2, 3, 1)) for each in (tile_block, tile_cells))

    packed, low, high, seen, footprint = project(
        plan, volume, footprint, block, cells, measured
    )
    below, above = shift_all(high, "slab", 1), shift_all(low, "slab", -1)
    chunks = shares(plan, packed, below, above)
    parts = [
        swap_all(chunks[flip], "xy", flip) if flip else chunks[0] for flip in reduce_order(bands)
    ]
    turned = turn(footprint)
    exact, rounded = correct(plan, seen, parts, turned)
    parts = [rounded] + [swap_all(rounded, "xy", flip) for flip in range(1, bands)]
    tiled = back_project(plan, volume, turned, block, cells, parts)

    line = [tiled] + [swap_all(tiled, "xy", flip) for flip in range(1, bands)]
    line = jnp.concatenate([each[:-1] for each in line] + [sum(each[-1:] for each in line)])
    chips = [line] + [swap_all(line, "slab", flip) for flip in range(2, slabs, 2)]
    chips += [swap_all(each, "slab", 1) for each in chips[::-1]]
    return smooth(volume, chips, exact, slabs, bands, footprint.shape[2])


def solution(mesh):
    placed = (
        P("slab", "xy", None),
        P("slab", "xy", None, None, None, None),
        P("slab", "xy", None, None),
        P("slab", "xy", None, None),
        P(),
    )
    return jax.shard_map(
        body,
        mesh=mesh,
        in_specs=placed,
        out_specs=(P("slab", "xy", None), P(None, ("slab", "xy"))),
        check_vma=False,
    )
```
